32 devices in a mesh: dp: 8 (over y, x, core), expert: 4 (over z).
Axes of the slice: x: 2, y: 2, z: 4, core: 2. Of those that a mesh axis runs over, the one named last changes fastest.
Arguments:
- layer_input: bfloat16 [8192, 1536], P(('dp', 'expert')), may hold values from -6 to 6
- gain_attn: float32 [1536], replicated, may hold values from 0.5 to 1.5
- w_qkv: bfloat16 [1536, 2560], replicated, may hold values from -0.15625 to 0.15625
- w_out: bfloat16 [1536, 1536], replicated, may hold values from -0.625 to 0.625
- gain_moe: float32 [1536], replicated, may hold values from 0.5 to 1.5
- w_gate_up: bfloat16 [20, 1536, 1024], P('expert'), may hold values from -0.15625 to 0.15625
- w_down: bfloat16 [20, 1536, 512], P('expert'), may hold values from -1 to 1
- doc_ids: int32 [32, 256], P(('dp', 'expert')), may hold values from 0 to 7, never falling along the last dimension, each value on 1 to 249 neighbouring positions
- routes: int32 [8192, 8], P(('dp', 'expert')), may hold values from 0 to 19, all different within a row; in each aligned block of 256 rows (0 to 255, 256 to 511, ...) at most 152 rows name the same one
- gates: float32 [8192, 8], P(('dp', 'expert')), may hold values from 0.08 to 0.25
- cotangent: bfloat16 [8192, 1536], P(('dp', 'expert')), may hold values from -6 to 6
Outputs:
- layer_output: bfloat16 [8192, 1536], P(('dp', 'expert'))
- grad_x: bfloat16 [8192, 1536], P(('dp', 'expert'))
- grad_gain_attn: float32 [1536], P(('dp', 'expert'))
- grad_w_qkv: float32 [1536, 2560], P(('dp', 'expert'))
- grad_w_out: float32 [1536, 1536], P(('dp', 'expert'))
- grad_gain_moe: float32 [1536], P(('dp', 'expert'))
- grad_w_gate_up: float32 [20, 1536, 1024], P('expert', 'dp')
- grad_w_down: float32 [20, 1536, 512], P('expert', 'dp')
The draws below stay inside these ranges and needn't reach their ends.
Inputs may be any that keep to these rules, and one draw needn't show every extreme that they name: `routes`: in each aligned block of 256 rows (the rows of one device) no expert is named by more than 152 rows, a bound that some block reaches. `doc_ids`: along each row the numbers never fall and every number of 0 to 7 appears; a document is a run of equal numbers of at most 249 tokens, and some document has exactly that many.
All inputs are finite; a program needn't handle non-finite values.
Results may differ from the reference program's by a relative error of at most 0.015.
Values may be sent and summed in bfloat16 or wider, within the bound.
A program may use at most 256 MiB of HBM per device.

```python
import math
import jax
import jax.numpy as jnp
import numpy as np
from jax import lax

D = 1536
HEADS = 24
KV = 8
HD = 64
FF = 512
TOP = 8
TOK_DEV = 256
DOC_IDS = 8
EXPERTS = 20
QKV = 2560
CAP = 152
TOKENS = 8192
N_DP = 8
N_EXPERT = 4


def spiked(entries, own_key, source, target, shards_of, factor):
    owner, partner = [(jnp.arange(entries.shape[axis_at]) // (entries.shape[axis_at] // shards_of)).reshape([-1 if axis == axis_at else 1 for axis in range(entries.ndim)]) for axis_at in (source, target)]
    chosen = jax.random.permutation(own_key, shards_of)[partner]
    strong = (owner == chosen) | (owner == (partner + shards_of // 2) % shards_of)
    return jnp.where(strong, factor * entries, entries)


def steps_of(key, dims, pieces, low, high):
    level = 1.0
    for dim, shards_of in pieces:
        heights = jax.random.uniform(jax.random.fold_in(jax.random.fold_in(key, 6), dim), (shards_of,), jnp.float32, low / len(pieces), high / len(pieces))
        level = level * jnp.repeat(jnp.exp(heights), dims[dim] // shards_of).reshape((-1,) + (1,) * (len(dims) - 1 - dim))
    return level


def split_up(amount, total, reach, lean):
    weights = [(1 << 20) // math.isqrt(rank ** lean) + 1 for rank in range(2, amount + 1)]
    rest, given = total - reach - (amount - 1), [1] * (amount - 1)
    while rest > 0:
        candidates = [i for i in range(amount - 1) if given[i] < reach]
        pool, left = sum([weights[i] for i in candidates]), rest
        for i in candidates:
            extra = min(reach - given[i], max(1, left * weights[i] // pool), rest)
            given[i] = given[i] + extra
            rest = rest - extra
    return np.array([reach] + given)


def ragged_sizes(rng, count, total, reach, slope):
    if count == 2:
        one = jax.random.randint(rng, (), max(1, total - reach), min(reach, total - 1) + 1)
        return jnp.stack([one, total - one])
    sizes = jnp.asarray(split_up(count, total, reach, slope), jnp.int32)
    pairs = (count - 1) // 2
    source_of, taker = sizes[1:1 + 2 * pairs:2], sizes[2:2 + 2 * pairs:2]
    room = jnp.minimum(source_of - 1, reach - taker)
    shifted = jax.random.randint(jax.random.fold_in(rng, 1), (pairs,), 0, 1 << 20) % (room + 1)
    sizes = sizes.at[1:1 + 2 * pairs:2].set(source_of - shifted).at[2:2 + 2 * pairs:2].set(taker + shifted)
    return sizes[jax.random.permutation(jax.random.fold_in(rng, 2), count)]


def routed_block(rng, own, number, rows, amount, top, limit, slope):
    order = jax.random.permutation(rng, amount)
    heavy_load, usual = load_shares(amount, rows * top, limit, slope, True), load_shares(amount, rows * top, limit, slope, False)
    places = jnp.arange(amount)

    def named(sizes, rotation):
        used = int((sizes > 0).sum())
        fixed = max(1, used // 4)
        shifted = fixed + (places - fixed + rotation * (used - fixed)) % max(1, amount - fixed)
        return jnp.zeros((amount,), jnp.int32).at[order[jnp.where(places < fixed, places, shifted)]].set(jnp.asarray(sizes, jnp.int32))

    sizes = jnp.where(number % 4 == 0, named(heavy_load, number // 4), named(usual, number - number // 4 - 1))
    mixed = jax.random.permutation(jax.random.fold_in(own, 3), amount)
    donor, taker = mixed[0:amount // 2 * 2:2], mixed[1:amount // 2 * 2:2]
    room = jnp.minimum(sizes[donor] - 1, limit - sizes[taker]) // 2
    room = jnp.where((donor == order[0]) | (taker == order[0]) | (sizes[taker] == 0), 0, jnp.maximum(room, 0))
    shifted = jax.random.randint(jax.random.fold_in(own, 4), (amount // 2,), 0, 1 << 20) % (room + 1)
    sizes = sizes.at[donor].add(-shifted).at[taker].add(shifted)
    labels = jnp.searchsorted(jnp.cumsum(sizes), jnp.arange(rows * top), side="right").astype(jnp.int32)
    listing = labels.reshape(top, rows).T
    listing = listing[jax.random.permutation(jax.random.fold_in(own, 1), rows)]
    rotation = jax.random.randint(jax.random.fold_in(own, 2), (rows, 1), 0, top)
    return jnp.take_along_axis(listing, (jnp.arange(top)[None, :] + rotation) % top, axis=1)


def load_shares(number_of, total, bound, skew, full):
    weights = [(1 << 20) // math.isqrt(grade ** skew) + 1 for grade in range(1, number_of + 1)]
    largest = bound if full else min(bound, max(-(-total // number_of), total * weights[0] // sum(weights)))
    least = 1 if total - largest >= number_of - 1 else 0
    holding, spare = [largest] + [least] * (number_of - 1), total - largest - least * (number_of - 1)
    while spare > 0:
        movable = [i for i in range(1, number_of) if holding[i] < largest] or [i for i in range(1, number_of) if holding[i] < bound]
        whole, budget = sum([weights[i] for i in movable]), spare
        for i in movable:
            more = min(bound - holding[i], max(1, budget * weights[i] // whole), spare)
            holding[i] = holding[i] + more
            spare = spare - more
    return np.array(holding)


def noise(key, extent, width, limit, pieces=(), held_as=jnp.bfloat16):
    drawn = width * jax.random.normal(key, extent, jnp.float32)
    if pieces:
        drawn = drawn * steps_of(key, extent, pieces, -0.22, 0.18)
    return jnp.clip(drawn, -limit, limit).astype(held_as)


def gaussian_with(own_key, shape, spread, bound, split, heavy, held_as=jnp.bfloat16):
    entries = spread * jax.random.normal(own_key, shape, jnp.float32)
    if split:
        entries = entries * steps_of(own_key, shape, split, -0.22, 0.18)
    return jnp.clip(spiked(entries, jax.random.fold_in(own_key, 3), *heavy), -bound, bound).astype(held_as)


def setup_inputs(seed: int = 0) -> dict:
    key_list = jax.random.split(jax.random.key(seed), 12)
    layer_input = gaussian_with(key_list[0], (TOKENS, D), 1.0, 6.0, ((0, 32),), (0, 1, 32, 2.75))
    gain_attn = jnp.clip(1.0 + 0.1 * jax.random.normal(key_list[1], (D,), jnp.float32), 0.5, 1.5)
    w_qkv = noise(key_list[2], (D, QKV), D ** -0.5, 0.15625)
    w_out = noise(key_list[3], (HEADS * HD, D), (D // 16) ** -0.5, 0.625)
    gain_moe = jnp.clip(1.0 + 0.1 * jax.random.normal(key_list[4], (D,), jnp.float32), 0.5, 1.5)
    w_gate_up = noise(key_list[5], (EXPERTS, D, 2 * FF), D ** -0.5, 0.15625, ((0, 4),))
    w_down = noise(key_list[6], (EXPERTS, D, FF), (FF // 16) ** -0.5, 1.0, ((0, 4),))
    doc_ids = jax.vmap(lambda own: jnp.searchsorted(jnp.cumsum(ragged_sizes(own, DOC_IDS, TOK_DEV, TOK_DEV - DOC_IDS + 1, 2)), jnp.arange(TOK_DEV), side="right"))(jax.random.split(key_list[7], (N_DP * N_EXPERT))).reshape((N_DP * N_EXPERT, TOK_DEV)).astype(jnp.int32)
    routes_keys = jax.random.split(jax.random.fold_in(key_list[8], 1), TOKENS // TOK_DEV)
    routes_turns = jax.random.permutation(jax.random.fold_in(key_list[8], 3), TOKENS // TOK_DEV)
    routes = jax.vmap(lambda own, number: routed_block(jax.random.fold_in(key_list[8], 2), own, number, TOK_DEV, EXPERTS, TOP, CAP, 1))(routes_keys, routes_turns).reshape((TOKENS, TOP))
    gates = jnp.clip(jnp.exp(math.log(0.25) - 1.1394343 * jax.random.uniform(key_list[9], (TOKENS, TOP), jnp.float32) ** steps_of(key_list[9], (TOKENS, TOP), ((0, 32),), -0.2, 0.2)), 0.08, 0.25)
    cotangent = noise(key_list[10], (TOKENS, D), 1.0, 6.0, ((0, 32),))
    return dict(layer_input=layer_input, gain_attn=gain_attn, w_qkv=w_qkv, w_out=w_out, gain_moe=gain_moe, w_gate_up=w_gate_up, w_down=w_down, doc_ids=doc_ids, routes=routes, gates=gates, cotangent=cotangent)


EPS = 1e-06
ROPE_BASE = 10000.0
MASKED = -1e+30

@jax.custom_vjp
def low(v):
    return lax.optimization_barrier(v.astype(jnp.bfloat16)).astype(jnp.float32)

@jax.custom_vjp
def low_back(v):
    return v

def low_keep(v):
    return (low(v), None)

def low_pass(kept, grad):
    return (grad,)

def back_keep(v):
    return (v, None)

def back_low(kept, grad):
    return (low(grad),)
low.defvjp(low_keep, low_pass)
low_back.defvjp(back_keep, back_low)

def precise(left, right):
    return jnp.dot(left, right, precision=lax.Precision.HIGHEST)

def rms_norm(value_rows, gain):
    return value_rows * lax.rsqrt(lax.optimization_barrier(jnp.mean(value_rows * value_rows, axis=-1, keepdims=True)) + EPS) * gain

def doc_positions(doc_row):
    row_index = jnp.arange(doc_row.shape[0], dtype=jnp.int32)
    before = jnp.concatenate([jnp.full((1,), -1, jnp.int32), doc_row[:-1]])
    starts = jnp.where(doc_row != before, row_index, 0)
    return row_index - lax.cummax(starts, axis=0)

def rope_tables(positions, head_size):
    half_size = head_size // 2
    inverse = ROPE_BASE ** (-(jnp.arange(half_size, dtype=jnp.float32) * 2.0 / head_size))
    angle_rows = positions.astype(jnp.float32)[:, None] * inverse[None, :]
    angle_rows = jnp.concatenate([angle_rows, angle_rows], axis=1)
    return (jnp.cos(angle_rows)[:, None, :], jnp.sin(angle_rows)[:, None, :])

def rotate(vectors, cos_t, sin_t):
    half_size = vectors.shape[-1] // 2
    turned = jnp.concatenate([-vectors[..., half_size:], vectors[..., :half_size]], axis=-1)
    return vectors * cos_t + turned * sin_t

def attend_block(normed, w_qkv, w_out, doc_row):
    tok_rows = normed.shape[0]
    group = HEADS // KV
    projected = low_back(precise(normed, w_qkv))
    query_rows = projected[:, :HEADS * HD].reshape(tok_rows, HEADS, HD)
    keys_raw = projected[:, HEADS * HD:(HEADS + KV) * HD].reshape(tok_rows, KV, HD)
    value_rows = low(projected[:, (HEADS + KV) * HD:].reshape(tok_rows, KV, HD))
    cos_t, sin_t = rope_tables(doc_positions(doc_row), HD)
    query_rows = low(rotate(query_rows, cos_t, sin_t)).reshape(tok_rows, KV, group, HD)
    rotated_keys = low(rotate(keys_raw, cos_t, sin_t))
    score_scale = 1.0 / math.sqrt(HD)
    unscaled_scores = jnp.einsum('uwbe,nwe->wbun', query_rows, rotated_keys, precision=lax.Precision.HIGHEST)
    scores = low_back(unscaled_scores * score_scale)
    row_index = jnp.arange(tok_rows, dtype=jnp.int32)
    allowed = (doc_row[:, None] == doc_row[None, :]) & (row_index[:, None] >= row_index[None, :])
    scores = jnp.where(allowed[None, None], scores, MASKED)
    attention_weights = low(jax.nn.softmax(scores, axis=-1))
    attention_result = jnp.einsum('qkwc,cqy->wqky', attention_weights, value_rows, precision=lax.Precision.HIGHEST)
    attention_result = low(low_back(attention_result.reshape(tok_rows, HEADS * HD)))
    return low_back(precise(attention_result, w_out))

def dispatch_table(routes):
    devices = N_DP * N_EXPERT
    flat_routes = routes.reshape(devices, TOK_DEV * TOP)
    onehot = (flat_routes[:, :, None] == jnp.arange(EXPERTS, dtype=jnp.int32)[None, None, :]).astype(jnp.int32)
    ranks = jnp.cumsum(onehot, axis=1) - 1
    slots = lax.optimization_barrier(jnp.sum(onehot * ranks, axis=2))
    blocks = jnp.arange(devices, dtype=jnp.int32)[:, None]
    pairs = blocks * (TOK_DEV * TOP) + jnp.arange(TOK_DEV * TOP, dtype=jnp.int32)[None, :]
    table = jnp.full((EXPERTS, devices * CAP), TOKENS * TOP, jnp.int32)
    return table.at[flat_routes, blocks * CAP + slots].set(pairs)

def forward(layer_in, gain_attn, w_qkv, w_out, gain_moe, w_gate_up, w_down, doc_ids, src_pairs, gates_pad):

    def one_block(carry, item):
        block_rows, doc_row = item
        normed = low(rms_norm(block_rows, gain_attn))
        return (carry, attend_block(normed, w_qkv, w_out, doc_row))
    blocks = layer_in.reshape(N_DP * N_EXPERT, TOK_DEV, D)
    _, attn = lax.scan(jax.checkpoint(one_block), jnp.zeros((), jnp.float32), (blocks, doc_ids))
    middle = layer_in + attn.reshape(TOKENS, D)
    normed_two = low(rms_norm(middle, gain_moe))
    padded_rows = jnp.concatenate([normed_two, jnp.zeros((1, D), jnp.float32)], axis=0)

    def one_expert(total, item):
        pairs, weight_gu, weight_dn = item
        token_of = pairs // TOP
        rows = low_back(padded_rows[token_of])
        gate_up = low_back(precise(rows, weight_gu))
        inner_act = low(jax.nn.silu(gate_up[:, :FF]) * gate_up[:, FF:])
        expert_out = low(low_back(precise(inner_act, weight_dn.T)))
        weights = gates_pad[pairs]
        return (total.at[token_of].add(weights[:, None] * expert_out), None)
    mixture, _ = lax.scan(jax.checkpoint(one_expert), jnp.zeros((TOKENS + 1, D), jnp.float32), (src_pairs, w_gate_up, w_down))
    return middle + mixture[:TOKENS]

def reference(layer_input, gain_attn, w_qkv, w_out, gain_moe, w_gate_up, w_down, doc_ids, routes, gates, cotangent):
    src_pairs = dispatch_table(routes)
    gates_pad = jnp.concatenate([gates.reshape(-1), jnp.zeros((1,), jnp.float32)])

    def layer(input_in, gain_one, qkv_in, out_in, gain_two, gu_in, dn_in):
        return forward(input_in, gain_one, qkv_in, out_in, gain_two, gu_in, dn_in, doc_ids, src_pairs, gates_pad)
    primal = (layer_input.astype(jnp.float32), gain_attn, w_qkv.astype(jnp.float32), w_out.astype(jnp.float32), gain_moe, w_gate_up.astype(jnp.float32), w_down.astype(jnp.float32))
    result, pull = jax.vjp(layer, *primal)
    grads = pull(cotangent.astype(jnp.float32))
    return (result.astype(jnp.bfloat16), grads[0].astype(jnp.bfloat16), grads[1], grads[2], grads[3], grads[4], grads[5], grads[6])
```

```python
import functools
import math

import jax
import jax.numpy as jnp
import numpy as np
from jax import lax
from jax.experimental import pallas as pl
from jax.experimental.pallas import tpu as pltpu
from jax.sharding import PartitionSpec as P

HEADS = 24
KV = 8
HD = 64


EPS = 1e-06
ROPE_BASE = 10000.0
MASKED = -1e30


MESH = pl.DeviceIdType.MESH
TABLE_ROWS = 16
COLUMN_TILE = 256
BACK_TILE = 512
CHUNK = 512
GAIN_ROWS = 128
ABSENT = -4096.0


def scatter_slots(table, hot_row, count, first=0):
    rank_row = table[hot_row : hot_row + 1, :]
    gate_row = table[8 + hot_row : 9 + hot_row, :]
    slots = lax.broadcasted_iota(jnp.int32, (count, rank_row.shape[1]), 0) + first
    hot = slots.astype(jnp.float32) == rank_row
    gate_col = jnp.sum(jnp.where(hot, gate_row, 0.0), axis=1, keepdims=True)
    return jnp.where(hot, 1.0, 0.0).astype(jnp.bfloat16), gate_col


def slot_table(routes_ref, gates_ref, n, exp_dev):
    tok, top = routes_ref.shape
    f32 = jnp.float32
    lane = lax.broadcasted_iota(jnp.int32, (tok, 128), 1)
    local = lax.rem(lane, 8)
    expert = lax.div(lane, TABLE_ROWS) * exp_dev + local
    expert = jnp.where((local < exp_dev) & (lane < n * TABLE_ROWS), expert, -1)
    member = jnp.zeros((tok, 128), f32)
    gate = jnp.zeros((tok, 128), f32)
    for c in range(top):
        hit = routes_ref[:, c : c + 1] == expert
        member = jnp.where(hit, 1.0, member)
        gate = jnp.where(hit, gates_ref[:, c : c + 1], gate)
    later = lax.broadcasted_iota(jnp.int32, (tok, tok), 0)
    earlier = lax.broadcasted_iota(jnp.int32, (tok, tok), 1)
    before = jnp.where(earlier < later, 1.0, 0.0).astype(jnp.bfloat16)
    rank = jnp.dot(before, member.astype(jnp.bfloat16), preferred_element_type=f32)
    rank = jnp.where(member > 0.0, rank, ABSENT)
    table = jnp.where(lax.rem(lane, TABLE_ROWS) < 8, rank, gate).T
    return table[0 : n * TABLE_ROWS, :]


def visible(doc_col, doc_row):
    tok = doc_col.shape[0]
    query = lax.broadcasted_iota(jnp.int32, (tok, tok), 0)
    key = lax.broadcasted_iota(jnp.int32, (tok, tok), 1)
    return (doc_col == doc_row) & (query >= key)


def rotary(doc_row, freq):
    doc_row = doc_row.astype(jnp.float32)
    doc_col = jnp.broadcast_to(doc_row, (128, doc_row.shape[1])).T[:, 0:1]
    mask = visible(doc_col, doc_row)
    position = jnp.sum(jnp.where(mask, 1.0, 0.0), axis=1, keepdims=True) - 1.0
    angle = position * freq
    return jnp.cos(angle), jnp.sin(angle), mask


def halves(values, sign):
    lane = lax.broadcasted_iota(jnp.int32, values.shape, 1)
    upper = pltpu.roll(values, 128 - HD // 2, 1)
    lower = pltpu.roll(values, HD // 2, 1)
    return jnp.where(lax.rem(lane, HD) < HD // 2, -sign * upper, sign * lower)


def heads_of(ref, first, count):
    cols = [ref[:, (first + h) * HD : (first + h + 1) * HD] for h in range(count)]
    return jnp.concatenate(cols, axis=0) if count > 1 else cols[0]


def masked_scores(q3, k1, mask3):
    dims = (((1,), (1,)), ((), ()))
    scores = lax.dot_general(q3, k1, dims, preferred_element_type=jnp.float32) * (1.0 / math.sqrt(HD))
    return jnp.where(mask3, scores, MASKED)


def softmax_parts(scores):
    top = jnp.max(scores, axis=1, keepdims=True)
    parts = jnp.exp(scores - top)
    return parts * (1.0 / jnp.sum(parts, axis=1, keepdims=True))


def inverse_rms(values):
    return lax.rsqrt(jnp.mean(values * values, axis=1, keepdims=True) + EPS)


def layer_kernel(n, exp_dev, cap_p, *refs):
    x_ref, cot_ref, wq_ref, wo_ref, wgu_ref, wd_ref = refs[:6]
    gain1_ref, gain2_ref, freq_ref, row_ref, routes_ref, gates_ref = refs[6:12]
    q_out, k_out, v_out, o_out, dx_ref, mix_ref, term_ref, land_ref, pair_gu, pair_d = refs[12:22]
    wgu, wd, xg, tabs, dyg, dgu, inner, rows, row_t, dxs, mixs = refs[22:33]
    own_sem, a_sem, w_sem, send_sem, recv_sem, back_send, back_recv, out_sem, mix_sem = refs[33:42]
    pair_send, pair_recv, plane_send, plane_recv, piece_sem = refs[42:]
    me = lax.axis_index("expert")
    core = lax.rem(lax.axis_index("dp"), 2)
    sibling = {"dp": lax.axis_index("dp") + 1 - 2 * core}
    n_dp, share = wgu.shape[1:3]
    half = n_dp // 2
    plane = lax.div(lax.axis_index("dp"), 2)
    tok, width = x_ref.shape
    hidden = inner.shape[1]
    rows_e = n * cap_p
    pair = 2 * cap_p
    second = exp_dev * pair
    f32 = jnp.float32
    bf = jnp.bfloat16

    def partner(side):
        value = lax.rem(lax.div(plane, 1 << side), 2)
        return plane + (1 - 2 * value) * (1 << side), value

    def load_gu(j):
        return pltpu.make_async_copy(wgu_ref.at[j], wgu.at[j], w_sem.at[0, j])

    def load_d(j):
        return pltpu.make_async_copy(wd_ref.at[j], wd.at[j], w_sem.at[1, j])

    own_dy = pltpu.make_async_copy(cot_ref, dyg.at[me], own_sem.at[0])
    own_x = pltpu.make_async_copy(x_ref, mixs, own_sem.at[1])
    load_q = [
        pltpu.make_async_copy(
            wq_ref.at[:, pl.ds(0, 2 * hidden)], dgu.at[pl.ds(0, width)], a_sem.at[0]
        ),
        pltpu.make_async_copy(
            wq_ref.at[:, pl.ds(2 * hidden, 2 * hidden)], dgu.at[pl.ds(width, width)], a_sem.at[1]
        ),
        pltpu.make_async_copy(
            wq_ref.at[:, pl.ds(4 * hidden, hidden)], inner.at[pl.ds(0, width)], a_sem.at[2]
        ),
    ]
    load_o = pltpu.make_async_copy(wo_ref, rows.at[pl.ds(0, width)], a_sem.at[3])
    own_dy.start()
    own_x.start()
    for copy in load_q:
        copy.start()
    load_o.start()
    for j in range(exp_dev):
        load_gu(j).start()
        load_d(j).start()

    barrier = pltpu.get_barrier_semaphore()
    for k in range(1, n):
        pl.semaphore_signal(
            barrier, inc=1, device_id={"expert": lax.rem(me + k, n)}, device_id_type=MESH
        )
    pl.semaphore_signal(barrier, inc=1, device_id=sibling, device_id_type=MESH)
    for side in range(2):
        pl.semaphore_signal(
            barrier, inc=1, device_id={"dp": 2 * partner(side)[0] + core}, device_id_type=MESH
        )
    pl.semaphore_wait(barrier, n + 2)

    moved = (tabs, xg, dyg)
    token_rows = (0, 1)
    cotangents = (2,)

    def hops(src, side, which):
        return [
            pltpu.make_async_remote_copy(
                src_ref=moved[kind].at[src],
                dst_ref=moved[kind].at[src],
                send_sem=send_sem.at[kind, side, src],
                recv_sem=recv_sem.at[kind, src],
                device_id={"expert": me + 2 * side - 1},
                device_id_type=MESH,
            )
            for kind in which
        ]

    def push(src, side, which):
        @pl.when(me < n - 1 if side else me > 0)
        def _():
            for copy in hops(src, side, which):
                copy.start()

    def push_own(which):
        push(me, 0, which)
        push(me, 1, which)

    def arrive(i, which):
        for side, src in ((1, me - i), (0, me + i)):

            @pl.when((src >= 0) & (src < n))
            def _():
                for copy in hops(src, side, which):
                    copy.wait_recv()
                push(src, side, which)

    own_dy.wait()
    push_own(cotangents)

    q_ref, o_ref, xn1 = dxs.at[0], dxs.at[1], dxs.at[3]
    k_ref = dxs.at[2, :, pl.ds(0, KV * HD)]
    v_ref = dxs.at[2, :, pl.ds(KV * HD, KV * HD)]
    group = HEADS // KV
    q_cols = HEADS * HD
    k_cols = KV * HD
    tabs[me] = slot_table(routes_ref, gates_ref, n, exp_dev)
    cos_t, sin_t, mask = rotary(row_ref[...], freq_ref[...])
    own_x.wait()
    h = mixs[...].astype(f32)
    xn1[...] = (h * inverse_rms(h) * gain1_ref[...]).astype(bf)
    for copy in load_q:
        copy.wait()
    for c in range(0, q_cols + 2 * k_cols, CHUNK):
        if c < 2 * hidden:
            w_cols = dgu[0:width, c : c + CHUNK]
        elif c < 4 * hidden:
            w_cols = dgu[width : 2 * width, c - 2 * hidden : c - 2 * hidden + CHUNK]
        else:
            w_cols = inner[0:width, c - 4 * hidden : c - 4 * hidden + CHUNK]
        proj = jnp.dot(xn1[...], w_cols, preferred_element_type=f32)
        for t in range(0, CHUNK, 128):
            tile = proj[:, t : t + 128]
            first = c + t
            if first < q_cols:
                tile = tile * cos_t + halves(tile, 1.0) * sin_t
                q_ref[:, first : first + 128] = tile.astype(bf)
            elif first < q_cols + k_cols:
                tile = tile * cos_t + halves(tile, 1.0) * sin_t
                k_ref[:, first - q_cols : first - q_cols + 128] = tile.astype(bf)
            else:
                first = first - q_cols - k_cols
                v_ref[:, first : first + 128] = tile.astype(bf)
    mask3 = jnp.concatenate([mask] * group, axis=0)
    for g in range(KV):
        q3 = heads_of(q_ref, g * group, group)
        weights = softmax_parts(masked_scores(q3, heads_of(k_ref, g, 1), mask3)).astype(bf)
        mixed = jnp.dot(weights, heads_of(v_ref, g, 1), preferred_element_type=f32).astype(bf)
        for s in range(group):
            first = (g * group + s) * HD
            o_ref[:, first : first + HD] = mixed[s * tok : (s + 1) * tok]
    kept = [
        pltpu.make_async_copy(src, dst, a_sem.at[4 + i])
        for i, (src, dst) in enumerate(
            ((q_ref, q_out), (k_ref, k_out), (v_ref, v_out), (o_ref, o_out))
        )
    ]
    for copy in kept:
        copy.start()
    load_o.wait()
    attended = jnp.dot(o_ref[...], rows[0:width, :], preferred_element_type=f32)
    h2 = mixs[...].astype(f32) + attended
    xg[me] = (h2 * inverse_rms(h2) * gain2_ref[...]).astype(bf)
    push_own(token_rows)
    arrive(1, cotangents)
    for copy in kept:
        copy.wait()

    def back(src):
        return pltpu.make_async_remote_copy(
            src_ref=dxs.at[src],
            dst_ref=dx_ref.at[me],
            send_sem=back_send.at[src],
            recv_sem=back_recv.at[me],
            device_id={"expert": src},
            device_id_type=MESH,
        )

    both = jnp.minimum(me, n - 1 - me)
    own_dx = pltpu.make_async_copy(dxs.at[me], dx_ref.at[me], own_sem.at[2])

    def source_of(i):
        paired = i <= 2 * both
        distance = jnp.where(paired, lax.div(i + 1, 2), i - both)
        go_left = jnp.where(paired, lax.rem(i, 2) == 1, 2 * me >= n - 1)
        return jnp.where(go_left, me - distance, me + distance)

    def mix_copy(i):
        return pltpu.make_async_copy(mixs, mix_ref.at[source_of(i)], mix_sem.at[0])

    def table_of(src):
        rows = pl.ds(pl.multiple_of(me * TABLE_ROWS, TABLE_ROWS), TABLE_ROWS)
        return tabs.at[src, rows, :]

    kinds = ((wgu, dgu, 0, 2 * hidden), (wd, inner, 2 * hidden, hidden))
    pair_land = (pair_gu, pair_d)
    cut = share // 2
    early = min(2, exp_dev - n // 2)
    spare = exp_dev * pair - rows_e

    def to_sibling(j):
        return [
            pltpu.make_async_remote_copy(
                src_ref=buf.at[j, pl.ds((1 - core) * half, half)],
                dst_ref=pair_land[kind].at[j],
                send_sem=pair_send.at[kind, j],
                recv_sem=pair_recv.at[kind, j],
                device_id=sibling,
                device_id_type=MESH,
            )
            for kind, (buf, *_) in enumerate(kinds)
        ]

    def term_copies(j):
        return [
            pltpu.make_async_copy(
                buf.at[j, pl.ds(core * half, half)],
                term_ref.at[:, j, :, pl.ds(start, wide)],
                out_sem.at[kind, j],
            )
            for kind, (buf, _, start, wide) in enumerate(kinds)
        ]

    def to_plane(j):
        copies = []
        for kind, (buf, _, start, wide) in enumerate(kinds):
            for side in range(2):
                target, value = partner(side)
                for t in range(half // 2):
                    low = t % (1 << side)
                    block = (t - low) * 2 + (1 - value) * (1 << side) + low
                    copies.append(
                        pltpu.make_async_remote_copy(
                            src_ref=buf.at[j, core * half + block, pl.ds(side * cut, cut)],
                            dst_ref=land_ref.at[side, t, j, :, pl.ds(start, wide)],
                            send_sem=plane_send.at[kind, side, t, j],
                            recv_sem=plane_recv.at[kind, side, t, j],
                            device_id={"dp": 2 * target + core},
                            device_id_type=MESH,
                        )
                    )
        return copies

    def finish(j):
        for kind, (buf, _, _, wide) in enumerate(kinds):
            to_sibling(j)[kind].wait_recv()
            pieces = [(b, c) for b in range(half) for c in range(0, wide, hidden)]
            loads = [
                pltpu.make_async_copy(
                    pair_land[kind].at[j, b, :, pl.ds(c, hidden)],
                    row_t.at[pl.ds(i * share, share), pl.ds(0, hidden)],
                    piece_sem.at[i],
                )
                for i, (b, c) in enumerate(pieces)
            ]
            for copy in loads:
                copy.start()
            for i, (b, c) in enumerate(pieces):
                loads[i].wait()
                other = row_t[i * share : (i + 1) * share, 0:hidden]
                buf[j, core * half + b, :, c : c + hidden] += other
        for copy in term_copies(j) + to_plane(j):
            copy.start()

    def form(j, between=None):
        def refill(src, carry):
            hot, gate_col = scatter_slots(table_of(src), j, cap_p)
            place = pl.ds(pl.multiple_of(spare + src * cap_p, 16), cap_p)
            rows[place, :] = jnp.dot(hot, xg[src], preferred_element_type=f32).astype(bf)
            place = pl.ds(pl.multiple_of(second + spare + src * cap_p, 16), cap_p)
            rows_dy = jnp.dot(hot, dyg[src], preferred_element_type=f32) * gate_col
            rows[place, :] = rows_dy.astype(bf)
            return carry

        lax.fori_loop(0, n, refill, 0)
        for store, cot, start, wide in kinds:
            base = spare if start == 0 else second + spare
            if start > 0 and between is not None:
                finish(between)
            for c in range(0, width, 128):
                row_t[c : c + 128, :] = rows[base : base + rows_e, c : c + 128].T
            for c in range(0, wide, COLUMN_TILE):
                cols = pl.ds(c, COLUMN_TILE)
                cots = cot[j * rows_e : (j + 1) * rows_e, cols]
                for low in range(0, n_dp, n_dp // 4):
                    some = row_t[low * share : (low + n_dp // 4) * share, :]
                    part = jnp.dot(some, cots, preferred_element_type=f32).astype(bf)
                    for r in range(low, low + n_dp // 4):
                        block = part[(r - low) * share : (r - low + 1) * share]
                        store[j, (r % 2) * half + r // 2, :, cols] = block
        for copy in to_sibling(j):
            copy.start()

    def one_pair(p, carry):
        arrive(2 * p + 1, token_rows)

        @pl.when(2 * p + 2 < n)
        def _():
            arrive(2 * p + 2, cotangents)

        sources = [source_of(2 * p), source_of(2 * p + 1)]
        for j in range(exp_dev):
            if j == exp_dev - 2:

                @pl.when(2 * p + 2 < n)
                def _():
                    arrive(2 * p + 2, token_rows)
                    arrive(2 * p + 3, cotangents)

            @pl.when(p == 0)
            def _():
                load_gu(j).wait()
                load_d(j).wait()

            gate_cols = []
            pair_a = pl.ds(j * pair, pair)
            pair_b = pl.ds(second + j * pair, pair)
            for s, src in enumerate(sources):
                here_a = pl.ds(j * pair + s * cap_p, cap_p)
                here_b = pl.ds(second + j * pair + s * cap_p, cap_p)
                hot, gate_col = scatter_slots(table_of(src), j, cap_p)
                gate_cols.append(gate_col)
                rows[here_a, :] = jnp.dot(hot, xg[src], preferred_element_type=f32).astype(bf)
                rows_dy = jnp.dot(hot, dyg[src], preferred_element_type=f32) * gate_col
                rows[here_b, :] = rows_dy.astype(bf)
            gate_col = jnp.concatenate(gate_cols, axis=0)
            w_in = wgu[j].reshape(width, 2 * hidden)
            w_out = wd[j].reshape(width, hidden)
            gate_up = jnp.dot(rows[pair_a, :], w_in, preferred_element_type=f32)
            inner_grad = jnp.dot(rows[pair_b, :], w_out, preferred_element_type=f32)
            gate_part = gate_up[:, :hidden]
            up_part = gate_up[:, hidden:]
            sig = jax.nn.sigmoid(gate_part)
            activated = gate_part * sig
            inner_act = (activated * up_part).astype(bf)
            grad_gate = inner_grad * up_part * sig * (1.0 + gate_part * (1.0 - sig))
            grad_up = inner_grad * activated
            grad_gu = jnp.concatenate([grad_gate, grad_up], axis=1).astype(bf)
            for s, src in enumerate(sources):
                place = pl.ds(pl.multiple_of(j * rows_e + src * cap_p, 16), cap_p)
                inner[place, :] = inner_act[s * cap_p : (s + 1) * cap_p]
                dgu[place, :] = grad_gu[s * cap_p : (s + 1) * cap_p]
            for c in range(0, width, BACK_TILE):
                rows_y = lax.dot_general(
                    inner_act,
                    w_out[c : c + BACK_TILE],
                    (((1,), (1,)), ((), ())),
                    preferred_element_type=f32,
                )
                rows[pair_a, pl.ds(c, BACK_TILE)] = (rows_y * gate_col).astype(bf)
            for c in range(0, width, BACK_TILE):
                rows_dx = lax.dot_general(
                    grad_gu,
                    w_in[c : c + BACK_TILE],
                    (((1,), (1,)), ((), ())),
                    preferred_element_type=f32,
                )
                rows[pair_b, pl.ds(c, BACK_TILE)] = rows_dx.astype(bf)
            if j <= early:

                @pl.when(p == n // 2 - 1)
                def _():
                    if j > 0:
                        finish(j - 1)
                    if j < early:
                        form(j)

        def hots_of(src):
            hots = [scatter_slots(table_of(src), j, cap_p)[0] for j in range(exp_dev)]
            return jnp.concatenate(hots, axis=0).T

        def slots_of(base, s, cols):
            parts = [rows[pl.ds(base + j * pair + s * cap_p, cap_p), cols] for j in range(exp_dev)]
            return jnp.concatenate(parts, axis=0)

        def outputs(s, hot_all):
            @pl.when(2 * p + s > 0)
            def _():
                mix_copy(2 * p + s - 1).wait()

            for c in range(0, width, COLUMN_TILE):
                cols = pl.ds(c, COLUMN_TILE)
                part = jnp.dot(hot_all, slots_of(0, s, cols), preferred_element_type=f32)
                mixs[:, cols] = part.astype(bf)
            mix_copy(2 * p + s).start()

        for s in (1, 0):
            src = sources[s]
            hot_all = hots_of(src)
            for c in range(0, width, COLUMN_TILE):
                cols = pl.ds(c, COLUMN_TILE)
                part = jnp.dot(hot_all, slots_of(second, s, cols), preferred_element_type=f32)
                dxs[src, :, cols] = part.astype(bf)
            if s == 0:

                @pl.when(p == 0)
                def _():
                    own_dx.start()

                @pl.when(p > 0)
                def _():
                    back(src).start()

                outputs(0, hot_all)
            else:
                back(src).start()
        outputs(1, hots_of(sources[1]))
        return carry

    lax.fori_loop(0, n // 2, one_pair, 0)

    for j in range(early, exp_dev):
        form(j, j - 1 if j > early else None)
    finish(exp_dev - 1)

    for k in range(1, n):
        peer = lax.rem(me + k, n)
        pltpu.make_async_remote_copy(
            src_ref=dxs.at[peer],
            dst_ref=dx_ref.at[peer],
            send_sem=back_send.at[peer],
            recv_sem=back_recv.at[peer],
            device_id={"expert": peer},
            device_id_type=MESH,
        ).wait_recv()
    for k in range(1, n):
        back(lax.rem(me + k, n)).wait_send()
    own_dx.wait()
    mix_copy(n - 1).wait()

    def settle(src, carry):
        for side in range(2):

            @pl.when(((src <= me) & (me < n - 1)) if side else ((src >= me) & (me > 0)))
            def _():
                for copy in hops(src, side, (0, 1, 2)):
                    copy.wait_send()

        return carry

    lax.fori_loop(0, n, settle, 0)
    for j in range(exp_dev):
        for copy in to_sibling(j) + to_plane(j):
            copy.wait_send()
        for copy in term_copies(j):
            copy.wait()
        for copy in to_plane(j):
            copy.wait_recv()


def run_layer(
    x, cot, w_qkv, w_out, w_gate_up, w_down, gain1, gain2, freq, doc_row, routes, gates, n, n_dp, capacity
):
    tok, width = x.shape
    exp_dev = w_gate_up.shape[0]
    hidden = w_down.shape[2]
    cap_p = -(-capacity // 16) * 16
    share = width // n_dp
    bf = jnp.bfloat16
    f32 = jnp.float32
    rows_e = n * cap_p
    spec = pl.BlockSpec(memory_space=pltpu.VMEM)
    any_spec = pl.BlockSpec(memory_space=pl.ANY)
    dma = pltpu.SemaphoreType.DMA
    macs = rows_e * exp_dev * width * hidden * 9 + tok * width * (w_qkv.shape[1] + width)
    shapes = (
        (tok, HEADS * HD),
        (tok, KV * HD),
        (tok, KV * HD),
        (tok, HEADS * HD),
        (n, tok, width),
        (n, tok, width),
        (n_dp // 2, exp_dev, share, 3 * hidden),
        (2, n_dp // 4, exp_dev, share // 2, 3 * hidden),
        (exp_dev, n_dp // 2, share, 2 * hidden),
        (exp_dev, n_dp // 2, share, hidden),
    )
    return pl.pallas_call(
        functools.partial(layer_kernel, n, exp_dev, cap_p),
        out_shape=tuple(jax.ShapeDtypeStruct(shape, bf) for shape in shapes),
        in_specs=[any_spec] * 6 + [spec] * 6,
        out_specs=(any_spec,) * len(shapes),
        scratch_shapes=[
            pltpu.VMEM((exp_dev, n_dp, share, 2 * hidden), bf),
            pltpu.VMEM((exp_dev, n_dp, share, hidden), bf),
            pltpu.VMEM((n, tok, width), bf),
            pltpu.VMEM((n, n * TABLE_ROWS, tok), f32),
            pltpu.VMEM((n, tok, width), bf),
            pltpu.VMEM((exp_dev * rows_e, 2 * hidden), bf),
            pltpu.VMEM((exp_dev * rows_e, hidden), bf),
            pltpu.VMEM((max(4 * exp_dev * cap_p, width), width), bf),
            pltpu.VMEM((width, rows_e), bf),
            pltpu.VMEM((n, tok, width), bf),
            pltpu.VMEM((tok, width), bf),
            dma((3,)),
            dma((8,)),
            dma((2, exp_dev)),
            dma((3, 2, n)),
            dma((3, n)),
            dma((n,)),
            dma((n,)),
            dma((2, exp_dev)),
            dma((1,)),
            dma((2, exp_dev)),
            dma((2, exp_dev)),
            dma((2, 2, n_dp // 4, exp_dev)),
            dma((2, 2, n_dp // 4, exp_dev)),
            dma((n_dp,)),
        ],
        compiler_params=pltpu.CompilerParams(
            collective_id=0, has_side_effects=True, vmem_limit_bytes=127 * 512 * 1024
        ),
        cost_estimate=pl.CostEstimate(
            flops=2 * macs,
            bytes_accessed=64 * 1024 * 1024,
            transcendentals=rows_e * exp_dev * hidden + HEADS * tok * tok,
        ),
    )(
        x,
        cot,
        w_qkv,
        w_out,
        w_gate_up.reshape(exp_dev, n_dp, share, 2 * hidden),
        w_down.reshape(exp_dev, n_dp, share, hidden),
        gain1,
        gain2,
        freq,
        doc_row,
        routes,
        gates,
    )


def tail_kernel(n, n_dp, exp_dev, *refs):
    dx_ref, mix_ref, term_ref, land_ref, wq_ref, wo_ref = refs[:6]
    dy_ref, x_ref, q_ref, k_ref, v_ref, o_ref = refs[6:12]
    freq_ref, row_ref, gain1_ref, gain2_ref = refs[12:16]
    gx_ref, h2_keep, r3, u3, y_land, own_last, got_last = refs[16:23]
    weight, parts, do, dqk, dh2_ref, gains, acc, got = refs[23:31]
    lhs, rhs, s1, r1, r2, s2, t1, u1, u2, t2 = refs[31:41]
    load_sem, piece_sem, y_send, y_recv, step_send, step_recv, out_sem, own_sem = refs[41:49]
    pair_send, pair_recv, dp_send, dp_recv, ex_send, ex_recv = refs[49:]
    dp = lax.axis_index("dp")
    me = lax.axis_index("expert")
    core = lax.rem(dp, 2)
    q = lax.div(dp, 2)
    half = n_dp // 2
    steps = half.bit_length() - 1
    f32 = jnp.float32
    bf = jnp.bfloat16
    tok, width = x_ref.shape
    rows = width // (n * n_dp)
    q_cols = HEADS * HD
    k_cols = KV * HD
    qkv = q_cols + 2 * k_cols
    out_chunks = width // CHUNK
    chunks = out_chunks + qkv // CHUNK
    ring = s1.shape[0]
    group = HEADS // KV
    scale = 1.0 / math.sqrt(HD)
    wide = (((1,), (1,)), ((), ()))
    tall = (((0,), (0,)), ((), ()))
    sibling = {"dp": dp + 1 - 2 * core}
    cut, span = acc.shape[3:]

    def value(bit):
        return lax.rem(lax.div(q, 1 << bit), 2)

    def across(bit):
        return {"dp": 2 * (q + (1 - 2 * value(bit)) * (1 << bit)) + core}

    def ex_peer(k):
        return lax.rem(me + k, n)

    batch = parts.shape[0] // tok
    h2_ref = dqk.at[:, pl.ds(0, width)]
    h2_out = pltpu.make_async_copy(h2_ref, h2_keep, load_sem.at[n + 2])

    def part_load(src, k):
        return pltpu.make_async_copy(src, parts.at[pl.ds(k % batch * tok, tok)], load_sem.at[k])

    def part(k):
        return parts[k % batch * tok : (k % batch + 1) * tok, :].astype(f32)

    dx_loads = [part_load(dx_ref.at[k], k) for k in range(n)]
    load_o = pltpu.make_async_copy(wo_ref, weight.at[:, pl.ds(0, width)], load_sem.at[n])
    load_q = pltpu.make_async_copy(wq_ref, weight, load_sem.at[n + 1])
    load_o.start()

    def kept_load(side, t):
        low = t % (1 << side)
        block = (t - low) * 2 + value(side) * (1 << side) + low
        return pltpu.make_async_copy(
            term_ref.at[block, :, pl.ds(side * cut, cut), :],
            acc.at[side, t],
            piece_sem.at[side, t, exp_dev],
        )

    def land_load(side, t, e):
        return pltpu.make_async_copy(
            land_ref.at[side, t, e],
            parts.at[pl.ds((t * exp_dev + e) * cut, cut)],
            piece_sem.at[side, t, e],
        )

    for side in range(2):
        for t in range(half // 2):
            kept_load(side, t).start()
    for t in range(half // 2):
        for e in range(exp_dev):
            land_load(0, t, e).start()

    barrier = pltpu.get_barrier_semaphore()
    pl.semaphore_signal(barrier, inc=1, device_id=sibling, device_id_type=MESH)
    for bit in range(steps):
        pl.semaphore_signal(barrier, inc=1, device_id=across(bit), device_id_type=MESH)
    for k in range(1, n):
        pl.semaphore_signal(
            barrier, inc=1, device_id={"expert": ex_peer(k)}, device_id_type=MESH
        )
    pl.semaphore_wait(barrier, 1 + steps + (n - 1))

    def y_copy(peer, slot):
        return pltpu.make_async_remote_copy(
            src_ref=mix_ref.at[peer],
            dst_ref=y_land.at[slot],
            send_sem=y_send.at[peer],
            recv_sem=y_recv.at[slot],
            device_id={"expert": peer},
            device_id_type=MESH,
        )

    for k in range(1, n):
        y_copy(ex_peer(k), me).start()

    def lands(side):
        return [land_load(side, t, e) for t in range(half // 2) for e in range(exp_dev)]

    def step_order(side):
        return [bit for bit in reversed(range(steps)) if bit != side]

    def step_start(side, s):
        order = step_order(side)[:s]
        return sum(value(bit) * (half >> (t + 2)) for t, bit in enumerate(order))

    def step_copy(side, s):
        bit = step_order(side)[s]
        size = half >> (s + 2)
        start = step_start(side, s) + (1 - value(bit)) * size
        return pltpu.make_async_remote_copy(
            src_ref=acc.at[side, start] if size == 1 else acc.at[side, pl.ds(start, size)],
            dst_ref=(
                got_last.at[side] if size == 1 else got.at[side, pl.ds(half // 2 - 2 * size, size)]
            ),
            send_sem=step_send.at[side, s],
            recv_sem=step_recv.at[side, s],
            device_id=across(bit),
            device_id_type=MESH,
        )

    def first_step(side):
        for t in range(half // 2):
            kept_load(side, t).wait()
        for copy in lands(side):
            copy.wait()
        for t in range(half // 2):
            for e in range(exp_dev):
                piece = parts[(t * exp_dev + e) * cut : (t * exp_dev + e + 1) * cut, :]
                acc[side, t, e] += piece
        step_copy(side, 0).start()

    def next_steps(side):
        for s in range(steps - 2):
            step_copy(side, s).wait_recv()
            size = half >> (s + 2)
            start = step_start(side, s + 1)
            for b in range(size):
                acc[side, start + b] += got[side, half // 2 - 2 * size + b]
            step_copy(side, s + 1).start()

    def own_share(side):
        start = step_start(side, steps - 1)
        return pltpu.make_async_copy(acc.at[side, start], own_last.at[side], out_sem.at[side])

    def bufs(c):
        if c is None:
            return t1, u1, u2, t2, u3, chunks
        return s1.at[c % ring], r1.at[c], r2.at[c], s2.at[c], r3.at[c], c

    def to_sibling(c):
        mine, landed, _, _, _, i = bufs(c)
        return pltpu.make_async_remote_copy(
            src_ref=mine.at[1 - core],
            dst_ref=landed,
            send_sem=pair_send.at[i],
            recv_sem=pair_recv.at[i],
            device_id=sibling,
            device_id_type=MESH,
        )

    def order_of(c):
        bits = list(range(steps))
        return bits[::-1] if c is not None and c % 2 else bits

    def position(place, c):
        order = order_of(c)
        return sum(((place >> bit) & 1) << (len(order) - 1 - s) for s, bit in enumerate(order))

    def start_of(c, s):
        order = order_of(c)
        return sum(value(bit) * (half >> (t + 1)) for t, bit in enumerate(order[:s]))

    def to_plane(c, s):
        mine, _, landed, _, _, i = bufs(c)
        bit = order_of(c)[s]
        size = half >> (s + 1)
        start = start_of(c, s) + (1 - value(bit)) * size
        return pltpu.make_async_remote_copy(
            src_ref=mine.at[core, pl.ds(start, size)],
            dst_ref=landed.at[pl.ds(half - 2 * size, size)],
            send_sem=dp_send.at[i, s],
            recv_sem=dp_recv.at[i, s],
            device_id=across(bit),
            device_id_type=MESH,
        )

    def to_expert(c, peer, slot):
        _, _, _, mine, landed, i = bufs(c)
        return pltpu.make_async_remote_copy(
            src_ref=mine.at[peer],
            dst_ref=landed.at[slot],
            send_sem=ex_send.at[i, peer],
            recv_sem=ex_recv.at[i, slot],
            device_id={"expert": peer},
            device_id_type=MESH,
        )

    def sent(c):
        to_sibling(c).wait_send()
        for s in range(steps):
            to_plane(c, s).wait_send()

    def place(c):
        if c is None:
            padding = jnp.zeros((GAIN_ROWS - gains.shape[0], width), f32)
            term = jnp.concatenate([gains[...], padding], axis=0).T
        else:
            if c >= ring:
                sent(c - ring)
            side = 0 if c < out_chunks else 1
            term = jnp.dot(lhs[side], rhs[c], preferred_element_type=f32)
        mine = bufs(c)[0]
        for b in range(n_dp * n):
            d, e = divmod(b, n)
            block = term[b * rows : (b + 1) * rows].astype(mine.dtype)
            mine[d % 2, position(d // 2, c), e, 0:rows, :] = block
        to_sibling(c).start()

    def pair_up(c):
        to_sibling(c).wait_recv()
        mine, landed = bufs(c)[:2]
        for b in range(half):
            mine[core, b] += landed[b]
        to_plane(c, 0).start()

    def halve(c, s):
        to_plane(c, s).wait_recv()
        mine, _, landed, summed = bufs(c)[:4]
        size = half >> (s + 1)
        start = start_of(c, s + 1)
        for b in range(size):
            both = mine[core, start + b] + landed[half - 2 * size + b]
            if s + 1 < steps:
                mine[core, start + b] = both
            else:
                summed[...] = both
        if s + 1 < steps:
            to_plane(c, s + 1).start()
        else:
            own_sum(c).start()
            for k in range(1, n):
                to_expert(c, ex_peer(k), me).start()

    def own_sum(c):
        summed, landed, i = bufs(c)[3:]
        return pltpu.make_async_copy(summed.at[me], landed.at[me], own_sem.at[i])

    def last(c):
        for k in range(1, n):
            to_expert(c, ex_peer(k), ex_peer(k)).wait_recv()

    first_step(0)
    for copy in lands(1):
        copy.start()
    gains[...] = jnp.zeros_like(gains)
    load_o.wait()
    for c in range(0, width, CHUNK):
        cols = slice(c, c + CHUNK)
        a = jnp.dot(o_ref[...], weight[:, cols], preferred_element_type=f32)
        h2_ref[:, cols] = x_ref[:, cols].astype(f32) + a
    h2_out.start()
    first_step(1)
    for copy in dx_loads[:batch]:
        copy.start()
    lhs[0] = o_ref[...].T
    for first in range(0, n, batch):
        for copy in dx_loads[first : first + batch]:
            if first > 0:
                copy.start()
        for copy in dx_loads[first : first + batch]:
            copy.wait()
        total = part(first)
        for k in range(first + 1, min(first + batch, n)):
            total = total + part(k)
        dh2_ref[...] = total if first == 0 else dh2_ref[...] + total
    h2 = h2_ref[...]
    dxn2 = dh2_ref[...]
    r2_col = inverse_rms(h2)
    gains[1:2, :] = jnp.sum(dxn2 * h2 * r2_col, axis=0, keepdims=True)
    w2 = dxn2 * gain2_ref[...]
    cubed = r2_col**3 * jnp.mean(w2 * h2, axis=1, keepdims=True)
    dh2_ref[...] = dy_ref[...].astype(f32) + r2_col * w2 - h2 * cubed
    for c in range(out_chunks):
        rhs[c] = dh2_ref[:, c * CHUNK : (c + 1) * CHUNK].astype(bf)
    for c in range(out_chunks):
        place(c)
    for c in range(0, q_cols, CHUNK):
        total = jnp.zeros((tok, CHUNK), f32)
        for d in range(out_chunks):
            total = total + lax.dot_general(
                rhs[d],
                weight[c : c + CHUNK, d * CHUNK : (d + 1) * CHUNK],
                wide,
                preferred_element_type=f32,
            )
        do[:, c : c + CHUNK] = total.astype(bf)
    load_q.start()
    for c in range(out_chunks):
        pair_up(c)

    h2_out.wait()
    cos_t, sin_t, mask = rotary(row_ref[...], freq_ref[...])
    mask3 = jnp.concatenate([mask] * group, axis=0)

    def put_proj(first, block):
        c, rest = divmod(first, CHUNK)
        rhs[out_chunks + c, :, rest : rest + block.shape[1]] = block

    for g in range(KV):
        q3 = heads_of(q_ref, g * group, group)
        k1 = heads_of(k_ref, g, 1)
        v1 = heads_of(v_ref, g, 1)
        do3 = heads_of(do, g * group, group)
        weights = softmax_parts(masked_scores(q3, k1, mask3))
        dpr = lax.dot_general(do3, v1, wide, preferred_element_type=f32)
        delta = jnp.sum(dpr * weights, axis=1, keepdims=True)
        ds = (weights * (dpr - delta)).astype(bf)
        dq = jnp.dot(ds, k1, preferred_element_type=f32) * scale
        for s in range(group):
            first = (g * group + s) * HD
            dqk[:, first : first + HD] = dq[s * tok : (s + 1) * tok]
        first = q_cols + g * HD
        dqk[:, first : first + HD] = (
            lax.dot_general(ds, q3, tall, preferred_element_type=f32) * scale
        )
        dv = lax.dot_general(weights.astype(bf), do3, tall, preferred_element_type=f32)
        put_proj(q_cols + k_cols + g * HD, dv.astype(bf))
    for c in range(0, q_cols + k_cols, 128):
        tile = dqk[:, c : c + 128]
        turned = halves(tile * sin_t, -1.0)
        put_proj(c, (tile * cos_t + turned).astype(bf))
    h = x_ref[...].astype(f32)
    r1_col = inverse_rms(h)
    lhs[1] = (h * r1_col * gain1_ref[...]).astype(bf).T

    def first_norm():
        load_q.wait()
        dxn1 = jnp.zeros((tok, width), f32)
        for c in range(out_chunks, chunks):
            first = (c - out_chunks) * CHUNK
            dxn1 = dxn1 + lax.dot_general(
                rhs[c], weight[:, first : first + CHUNK], wide, preferred_element_type=f32
            )
        x = x_ref[...].astype(f32)
        gains[0:1, :] = jnp.sum(dxn1 * x * r1_col, axis=0, keepdims=True)
        w1 = dxn1 * gain1_ref[...]
        cubed = r1_col**3 * jnp.mean(w1 * x, axis=1, keepdims=True)
        gx_ref[...] = (dh2_ref[...] + r1_col * w1 - x * cubed).astype(bf)

    line = list(range(chunks)) + [None]
    late = line[out_chunks:]
    for tick in range(len(line) + steps):
        for s in reversed(range(steps)):
            if 0 <= tick - s < len(line):
                halve(line[tick - s], s)
        if tick < len(late):
            place(late[tick])
        if 1 <= tick <= len(late):
            pair_up(late[tick - 1])
        if 0 <= tick - steps < len(line):
            last(line[tick - steps])
        if tick == 1:
            first_norm()
        if tick == 3:
            for side in range(2):
                next_steps(side)
                own_share(side).start()

    for c in line:
        if c is None or c >= chunks - ring:
            sent(c)
        for k in range(1, n):
            to_expert(c, ex_peer(k), me).wait_send()
    for c in line:
        own_sum(c).wait()
    for side in range(2):
        for s in range(steps - 1):
            step_copy(side, s).wait_send()
        step_copy(side, steps - 2).wait_recv()
        own_share(side).wait()
    for k in range(1, n):
        y_copy(ex_peer(k), ex_peer(k)).wait_recv()
        y_copy(ex_peer(k), me).wait_send()


def run_tail(
    dx_parts, mix_parts, term, landed, w_qkv, w_out, dy, x, q, k, v, o, freq, doc_row, gain1, gain2, n, n_dp
):
    tok, width = x.shape
    exp_dev = term.shape[1]
    cut, span = landed.shape[3:]
    qkv = w_qkv.shape[1]
    rows = width // (n * n_dp)
    rows_p = -(-rows // 16) * 16
    half = n_dp // 2
    steps = half.bit_length() - 1
    chunks = (width + qkv) // CHUNK
    ring = steps + 2
    lanes = GAIN_ROWS
    bf = jnp.bfloat16
    f32 = jnp.float32
    dma = pltpu.SemaphoreType.DMA
    spec = pl.BlockSpec(memory_space=pltpu.VMEM)
    any_spec = pl.BlockSpec(memory_space=pl.ANY)
    return pl.pallas_call(
        functools.partial(tail_kernel, n, n_dp, exp_dev),
        out_shape=(
            jax.ShapeDtypeStruct((tok, width), bf),
            jax.ShapeDtypeStruct((tok, width), f32),
            jax.ShapeDtypeStruct((chunks, n, rows_p, CHUNK), bf),
            jax.ShapeDtypeStruct((n, rows_p, lanes), f32),
            jax.ShapeDtypeStruct((n, tok, width), bf),
            jax.ShapeDtypeStruct((2, exp_dev, cut, span), bf),
            jax.ShapeDtypeStruct((2, exp_dev, cut, span), bf),
        ),
        in_specs=[any_spec] * 6 + [spec] * 10,
        out_specs=(spec,) + (any_spec,) * 6,
        scratch_shapes=[
            pltpu.VMEM((width, qkv), bf),
            pltpu.VMEM((min(n, 4) * tok, width), bf),
            pltpu.VMEM((tok, HEADS * HD), bf),
            pltpu.VMEM((tok, (HEADS + KV) * HD), f32),
            pltpu.VMEM((tok, width), f32),
            pltpu.VMEM((8, width), f32),
            pltpu.VMEM((2, half // 2, exp_dev, cut, span), bf),
            pltpu.VMEM((2, max(half // 2 - 2, 1), exp_dev, cut, span), bf),
            pltpu.VMEM((2, width, tok), bf),
            pltpu.VMEM((chunks, tok, CHUNK), bf),
            pltpu.VMEM((ring, 2, half, n, rows_p, CHUNK), bf),
            pltpu.VMEM((chunks, half, n, rows_p, CHUNK), bf),
            pltpu.VMEM((chunks, half - 1, n, rows_p, CHUNK), bf),
            pltpu.VMEM((chunks, n, rows_p, CHUNK), bf),
            pltpu.VMEM((2, half, n, rows_p, lanes), f32),
            pltpu.VMEM((half, n, rows_p, lanes), f32),
            pltpu.VMEM((half - 1, n, rows_p, lanes), f32),
            pltpu.VMEM((n, rows_p, lanes), f32),
            dma((n + 3,)),
            dma((2, half // 2, exp_dev + 1)),
            dma((n,)),
            dma((n,)),
            dma((2, steps)),
            dma((2, steps)),
            dma((2,)),
            dma((chunks + 1,)),
            dma((chunks + 1,)),
            dma((chunks + 1,)),
            dma((chunks + 1, steps)),
            dma((chunks + 1, steps)),
            dma((chunks + 1, n)),
            dma((chunks + 1, n)),
        ],
        compiler_params=pltpu.CompilerParams(
            collective_id=1, has_side_effects=True, vmem_limit_bytes=127 * 512 * 1024
        ),
        cost_estimate=pl.CostEstimate(
            flops=2 * tok * width * (3 * qkv + 3 * width),
            bytes_accessed=64 * 1024 * 1024,
            transcendentals=HEADS * tok * tok,
        ),
    )(dx_parts, mix_parts, term, landed, w_qkv, w_out, dy, x, q, k, v, o, freq, doc_row, gain1, gain2)


def shards(
    layer_input,
    gain_attn,
    w_qkv,
    w_out,
    gain_moe,
    w_gate_up,
    w_down,
    doc_ids,
    routes,
    gates,
    cotangent,
):
    tok_rows, model_width = layer_input.shape
    exp_dev = w_gate_up.shape[0]
    top_count = routes.shape[1]
    owners = lax.axis_size("expert")
    n_dp = lax.axis_size("dp")
    n_experts = exp_dev * owners
    capacity = 8 * (3 * tok_rows * top_count // (16 * n_experts))
    lane = np.arange(128) % (HD // 2)
    freq = jnp.asarray((ROPE_BASE ** (-(lane * 2.0 / HD)))[None].astype(np.float32))
    gain1 = gain_attn.reshape(1, model_width)
    gain2 = gain_moe.reshape(1, model_width)
    q, k, v, attended, grad_partial, mix_partial, term, landed, *_ = run_layer(
        layer_input,
        cotangent,
        w_qkv,
        w_out,
        w_gate_up,
        w_down,
        gain1,
        gain2,
        freq,
        doc_ids,
        routes,
        gates,
        owners,
        n_dp,
        capacity,
    )
    grad_x, middle, dense, gain_parts, mix_landed, own_share, got_share = run_tail(
        grad_partial,
        mix_partial,
        term,
        landed,
        w_qkv,
        w_out,
        cotangent,
        layer_input,
        q,
        k,
        v,
        attended,
        freq,
        doc_ids,
        gain1,
        gain2,
        owners,
        n_dp,
    )
    f32 = jnp.float32
    me = lax.axis_index("expert")
    hidden = w_down.shape[2]
    share_rows = model_width // (owners * n_dp)
    out_chunks = model_width // CHUNK
    mixture = lax.dynamic_index_in_dim(mix_partial, me, 0, keepdims=False).astype(f32)
    for k in range(1, owners):
        peer = (me + k) % owners
        mixture = mixture + lax.dynamic_index_in_dim(mix_landed, peer, 0, keepdims=False).astype(f32)
    layer_output = (middle + mixture).astype(jnp.bfloat16)
    dense = jnp.sum(dense[:, :, :share_rows].astype(f32), axis=1).transpose(1, 0, 2)
    gain_share = jnp.sum(gain_parts[:, :share_rows], axis=0)
    experts = own_share.astype(f32) + got_share.astype(f32)
    experts = jnp.concatenate([experts[0], experts[1]], axis=1)
    return (
        layer_output,
        grad_x,
        gain_share[:, 0],
        dense[:, out_chunks:].reshape(share_rows, -1),
        dense[:, :out_chunks].reshape(share_rows, -1),
        gain_share[:, 1],
        experts[..., : 2 * hidden],
        experts[..., 2 * hidden :],
    )


def solution(mesh):
    in_specs = (
        P(("dp", "expert"), None),
        P(),
        P(),
        P(),
        P(),
        P("expert", None, None),
        P("expert", None, None),
        P(("dp", "expert"), None),
        P(("dp", "expert"), None),
        P(("dp", "expert"), None),
        P(("dp", "expert"), None),
    )
    out_specs = (
        P(("dp", "expert"), None),
        P(("dp", "expert"), None),
        P(("dp", "expert")),
        P(("dp", "expert"), None),
        P(("dp", "expert"), None),
        P(("dp", "expert")),
        P("expert", "dp", None),
        P("expert", "dp", None),
    )
    return jax.shard_map(shards, mesh=mesh, in_specs=in_specs, out_specs=out_specs, check_vma=False)
```

```python
import functools
import math

import jax
import jax.numpy as jnp
import numpy as np
from jax import lax
from jax.experimental import pallas as pl
from jax.experimental.pallas import tpu as pltpu
from jax.sharding import PartitionSpec as P

HEADS = 24
KV = 8
HD = 64


EPS = 1e-06
ROPE_BASE = 10000.0
MASKED = -1e30


MESH = pl.DeviceIdType.MESH
TABLE_ROWS = 16
COLUMN_TILE = 256
BACK_TILE = 512
CHUNK = 512
GAIN_ROWS = 128
ABSENT = -4096.0


def scatter_slots(table, hot_row, count, first=0):
    rank_row = table[hot_row : hot_row + 1, :]
    gate_row = table[8 + hot_row : 9 + hot_row, :]
    slots = lax.broadcasted_iota(jnp.int32, (count, rank_row.shape[1]), 0) + first
    hot = slots.astype(jnp.float32) == rank_row
    gate_col = jnp.sum(jnp.where(hot, gate_row, 0.0), axis=1, keepdims=True)
    return jnp.where(hot, 1.0, 0.0).astype(jnp.bfloat16), gate_col


def slot_table(routes_ref, gates_ref, n, exp_dev):
    top, tok = routes_ref.shape
    f32 = jnp.float32
    facts = [routes_ref[...].astype(f32), gates_ref[...], jnp.zeros((128 - 2 * top, tok), f32)]
    facts = jnp.concatenate(facts, axis=0).T
    lane = lax.broadcasted_iota(jnp.int32, (tok, 128), 1)
    local = lax.rem(lane, 8)
    expert = lax.div(lane, TABLE_ROWS) * exp_dev + local
    expert = jnp.where((local < exp_dev) & (lane < n * TABLE_ROWS), expert, -1).astype(f32)
    member = jnp.zeros((tok, 128), f32)
    gate = jnp.zeros((tok, 128), f32)
    for c in range(top):
        hit = facts[:, c : c + 1] == expert
        member = jnp.where(hit, 1.0, member)
        gate = jnp.where(hit, facts[:, top + c : top + c + 1], gate)
    later = lax.broadcasted_iota(jnp.int32, (tok, tok), 0)
    earlier = lax.broadcasted_iota(jnp.int32, (tok, tok), 1)
    before = jnp.where(earlier < later, 1.0, 0.0).astype(jnp.bfloat16)
    rank = jnp.dot(before, member.astype(jnp.bfloat16), preferred_element_type=f32)
    rank = jnp.where(member > 0.0, rank, ABSENT)
    table = jnp.where(lax.rem(lane, TABLE_ROWS) < 8, rank, gate).T
    return table[0 : n * TABLE_ROWS, :]


def visible(doc_col, doc_row):
    tok = doc_col.shape[0]
    query = lax.broadcasted_iota(jnp.int32, (tok, tok), 0)
    key = lax.broadcasted_iota(jnp.int32, (tok, tok), 1)
    return (doc_col == doc_row) & (query >= key)


def rotary(doc_row, freq):
    doc_row = doc_row.astype(jnp.float32)
    doc_col = jnp.broadcast_to(doc_row, (128, doc_row.shape[1])).T[:, 0:1]
    mask = visible(doc_col, doc_row)
    position = jnp.sum(jnp.where(mask, 1.0, 0.0), axis=1, keepdims=True) - 1.0
    angle = position * freq
    return jnp.cos(angle), jnp.sin(angle), mask


def halves(values, sign):
    lane = lax.broadcasted_iota(jnp.int32, values.shape, 1)
    upper = pltpu.roll(values, 128 - HD // 2, 1)
    lower = pltpu.roll(values, HD // 2, 1)
    return jnp.where(lax.rem(lane, HD) < HD // 2, -sign * upper, sign * lower)


def heads_of(ref, first, count):
    cols = [ref[:, (first + h) * HD : (first + h + 1) * HD] for h in range(count)]
    return jnp.concatenate(cols, axis=0) if count > 1 else cols[0]


def masked_scores(q3, k1, mask3):
    dims = (((1,), (1,)), ((), ()))
    scores = lax.dot_general(q3, k1, dims, preferred_element_type=jnp.float32) * (1.0 / math.sqrt(HD))
    return jnp.where(mask3, scores, MASKED)


def softmax_parts(scores):
    top = jnp.max(scores, axis=1, keepdims=True)
    parts = jnp.exp(scores - top)
    return parts * (1.0 / jnp.sum(parts, axis=1, keepdims=True))


def inverse_rms(values):
    return lax.rsqrt(jnp.mean(values * values, axis=1, keepdims=True) + EPS)


def layer_kernel(n, exp_dev, cap_p, *refs):
    x_ref, cot_ref, wq_ref, wo_ref, wgu_ref, wd_ref = refs[:6]
    gain1_ref, gain2_ref, freq_ref, row_ref, routes_ref, gates_ref = refs[6:12]
    q_out, k_out, v_out, o_out, dx_ref, mix_ref, term_ref, land_ref, pair_gu, pair_d = refs[12:22]
    wgu, wd, xg, tabs, dyg, dgu, inner, rows, row_t, dxs, mixs = refs[22:33]
    own_sem, a_sem, w_sem, send_sem, recv_sem, back_send, back_recv, out_sem, mix_sem = refs[33:42]
    pair_send, pair_recv, plane_send, plane_recv, piece_sem = refs[42:]
    me = lax.axis_index("expert")
    core = lax.rem(lax.axis_index("dp"), 2)
    sibling = {"dp": lax.axis_index("dp") + 1 - 2 * core}
    n_dp, share = wgu.shape[1:3]
    half = n_dp // 2
    plane = lax.div(lax.axis_index("dp"), 2)
    tok, width = x_ref.shape
    hidden = inner.shape[1]
    rows_e = n * cap_p
    pair = 2 * cap_p
    second = exp_dev * pair
    f32 = jnp.float32
    bf = jnp.bfloat16

    def partner(side):
        value = lax.rem(lax.div(plane, 1 << side), 2)
        return plane + (1 - 2 * value) * (1 << side), value

    def load_gu(j):
        return pltpu.make_async_copy(wgu_ref.at[j], wgu.at[j], w_sem.at[0, j])

    def load_d(j):
        return pltpu.make_async_copy(wd_ref.at[j], wd.at[j], w_sem.at[1, j])

    own_dy = pltpu.make_async_copy(cot_ref, dyg.at[me], own_sem.at[0])
    own_x = pltpu.make_async_copy(x_ref, mixs, own_sem.at[1])
    load_q = [
        pltpu.make_async_copy(
            wq_ref.at[:, pl.ds(0, 2 * hidden)], dgu.at[pl.ds(0, width)], a_sem.at[0]
        ),
        pltpu.make_async_copy(
            wq_ref.at[:, pl.ds(2 * hidden, 2 * hidden)], dgu.at[pl.ds(width, width)], a_sem.at[1]
        ),
        pltpu.make_async_copy(
            wq_ref.at[:, pl.ds(4 * hidden, hidden)], inner.at[pl.ds(0, width)], a_sem.at[2]
        ),
    ]
    load_o = pltpu.make_async_copy(wo_ref, rows.at[pl.ds(0, width)], a_sem.at[3])
    own_dy.start()
    own_x.start()
    for copy in load_q:
        copy.start()
    load_o.start()
    for j in range(exp_dev):
        load_gu(j).start()
        load_d(j).start()

    barrier = pltpu.get_barrier_semaphore()
    for k in range(1, n):
        pl.semaphore_signal(
            barrier, inc=1, device_id={"expert": lax.rem(me + k, n)}, device_id_type=MESH
        )
    pl.semaphore_signal(barrier, inc=1, device_id=sibling, device_id_type=MESH)
    for side in range(2):
        pl.semaphore_signal(
            barrier, inc=1, device_id={"dp": 2 * partner(side)[0] + core}, device_id_type=MESH
        )
    pl.semaphore_wait(barrier, n + 2)

    moved = (tabs, xg, dyg)
    token_rows = (0, 1)
    cotangents = (2,)

    def hops(src, side, which):
        return [
            pltpu.make_async_remote_copy(
                src_ref=moved[kind].at[src],
                dst_ref=moved[kind].at[src],
                send_sem=send_sem.at[kind, side, src],
                recv_sem=recv_sem.at[kind, src],
                device_id={"expert": me + 2 * side - 1},
                device_id_type=MESH,
            )
            for kind in which
        ]

    def push(src, side, which):
        @pl.when(me < n - 1 if side else me > 0)
        def _():
            for copy in hops(src, side, which):
                copy.start()

    def push_own(which):
        push(me, 0, which)
        push(me, 1, which)

    def arrive(i, which):
        for side, src in ((1, me - i), (0, me + i)):

            @pl.when((src >= 0) & (src < n))
            def _():
                for copy in hops(src, side, which):
                    copy.wait_recv()
                push(src, side, which)

    own_dy.wait()
    push_own(cotangents)

    q_ref, o_ref, xn1 = dxs.at[0], dxs.at[1], dxs.at[3]
    k_ref = dxs.at[2, :, pl.ds(0, KV * HD)]
    v_ref = dxs.at[2, :, pl.ds(KV * HD, KV * HD)]
    group = HEADS // KV
    q_cols = HEADS * HD
    k_cols = KV * HD
    tabs[me] = slot_table(routes_ref, gates_ref, n, exp_dev)
    cos_t, sin_t, mask = rotary(row_ref[...], freq_ref[...])
    own_x.wait()
    h = mixs[...].astype(f32)
    xn1[...] = (h * inverse_rms(h) * gain1_ref[...]).astype(bf)
    for copy in load_q:
        copy.wait()
    for c in range(0, q_cols + 2 * k_cols, CHUNK):
        if c < 2 * hidden:
            w_cols = dgu[0:width, c : c + CHUNK]
        elif c < 4 * hidden:
            w_cols = dgu[width : 2 * width, c - 2 * hidden : c - 2 * hidden + CHUNK]
        else:
            w_cols = inner[0:width, c - 4 * hidden : c - 4 * hidden + CHUNK]
        proj = jnp.dot(xn1[...], w_cols, preferred_element_type=f32)
        for t in range(0, CHUNK, 128):
            tile = proj[:, t : t + 128]
            first = c + t
            if first < q_cols:
                tile = tile * cos_t + halves(tile, 1.0) * sin_t
                q_ref[:, first : first + 128] = tile.astype(bf)
            elif first < q_cols + k_cols:
                tile = tile * cos_t + halves(tile, 1.0) * sin_t
                k_ref[:, first - q_cols : first - q_cols + 128] = tile.astype(bf)
            else:
                first = first - q_cols - k_cols
                v_ref[:, first : first + 128] = tile.astype(bf)
    mask3 = jnp.concatenate([mask] * group, axis=0)
    for g in range(KV):
        q3 = heads_of(q_ref, g * group, group)
        weights = softmax_parts(masked_scores(q3, heads_of(k_ref, g, 1), mask3)).astype(bf)
        mixed = jnp.dot(weights, heads_of(v_ref, g, 1), preferred_element_type=f32).astype(bf)
        for s in range(group):
            first = (g * group + s) * HD
            o_ref[:, first : first + HD] = mixed[s * tok : (s + 1) * tok]
    kept = [
        pltpu.make_async_copy(src, dst, a_sem.at[4 + i])
        for i, (src, dst) in enumerate(
            ((q_ref, q_out), (k_ref, k_out), (v_ref, v_out), (o_ref, o_out))
        )
    ]
    for copy in kept:
        copy.start()
    load_o.wait()
    attended = jnp.dot(o_ref[...], rows[0:width, :], preferred_element_type=f32)
    h2 = mixs[...].astype(f32) + attended
    xg[me] = (h2 * inverse_rms(h2) * gain2_ref[...]).astype(bf)
    push_own(token_rows)
    arrive(1, cotangents)
    for copy in kept:
        copy.wait()

    def back(src):
        return pltpu.make_async_remote_copy(
            src_ref=dxs.at[src],
            dst_ref=dx_ref.at[me],
            send_sem=back_send.at[src],
            recv_sem=back_recv.at[me],
            device_id={"expert": src},
            device_id_type=MESH,
        )

    both = jnp.minimum(me, n - 1 - me)
    own_dx = pltpu.make_async_copy(dxs.at[me], dx_ref.at[me], own_sem.at[2])

    def source_of(i):
        paired = i <= 2 * both
        distance = jnp.where(paired, lax.div(i + 1, 2), i - both)
        go_left = jnp.where(paired, lax.rem(i, 2) == 1, 2 * me >= n - 1)
        return jnp.where(go_left, me - distance, me + distance)

    def mix_copy(i):
        return pltpu.make_async_copy(mixs, mix_ref.at[source_of(i)], mix_sem.at[0])

    def table_of(src):
        rows = pl.ds(pl.multiple_of(me * TABLE_ROWS, TABLE_ROWS), TABLE_ROWS)
        return tabs.at[src, rows, :]

    kinds = ((wgu, dgu, 0, 2 * hidden), (wd, inner, 2 * hidden, hidden))
    pair_land = (pair_gu, pair_d)
    cut = share // 2
    early = min(2, exp_dev - n // 2)
    spare = exp_dev * pair - rows_e

    def to_sibling(j):
        return [
            pltpu.make_async_remote_copy(
                src_ref=buf.at[j, pl.ds((1 - core) * half, half)],
                dst_ref=pair_land[kind].at[j],
                send_sem=pair_send.at[kind, j],
                recv_sem=pair_recv.at[kind, j],
                device_id=sibling,
                device_id_type=MESH,
            )
            for kind, (buf, *_) in enumerate(kinds)
        ]

    def term_copies(j):
        return [
            pltpu.make_async_copy(
                buf.at[j, pl.ds(core * half, half)],
                term_ref.at[:, j, :, pl.ds(start, wide)],
                out_sem.at[kind, j],
            )
            for kind, (buf, _, start, wide) in enumerate(kinds)
        ]

    def to_plane(j):
        copies = []
        for kind, (buf, _, start, wide) in enumerate(kinds):
            for side in range(2):
                target, value = partner(side)
                for t in range(half // 2):
                    low = t % (1 << side)
                    block = (t - low) * 2 + (1 - value) * (1 << side) + low
                    copies.append(
                        pltpu.make_async_remote_copy(
                            src_ref=buf.at[j, core * half + block, pl.ds(side * cut, cut)],
                            dst_ref=land_ref.at[side, t, j, :, pl.ds(start, wide)],
                            send_sem=plane_send.at[kind, side, t, j],
                            recv_sem=plane_recv.at[kind, side, t, j],
                            device_id={"dp": 2 * target + core},
                            device_id_type=MESH,
                        )
                    )
        return copies

    def finish(j):
        for kind, (buf, _, _, wide) in enumerate(kinds):
            to_sibling(j)[kind].wait_recv()
            pieces = [(b, c) for b in range(half) for c in range(0, wide, hidden)]
            loads = [
                pltpu.make_async_copy(
                    pair_land[kind].at[j, b, :, pl.ds(c, hidden)],
                    row_t.at[pl.ds(i * share, share), pl.ds(0, hidden)],
                    piece_sem.at[i],
                )
                for i, (b, c) in enumerate(pieces)
            ]
            for copy in loads:
                copy.start()
            for i, (b, c) in enumerate(pieces):
                loads[i].wait()
                other = row_t[i * share : (i + 1) * share, 0:hidden]
                buf[j, core * half + b, :, c : c + hidden] += other
        for copy in term_copies(j) + to_plane(j):
            copy.start()

    def form(j, between=None):
        def refill(src, carry):
            hot, gate_col = scatter_slots(table_of(src), j, cap_p)
            place = pl.ds(pl.multiple_of(spare + src * cap_p, 16), cap_p)
            rows[place, :] = jnp.dot(hot, xg[src], preferred_element_type=f32).astype(bf)
            place = pl.ds(pl.multiple_of(second + spare + src * cap_p, 16), cap_p)
            rows_dy = jnp.dot(hot, dyg[src], preferred_element_type=f32) * gate_col
            rows[place, :] = rows_dy.astype(bf)
            return carry

        lax.fori_loop(0, n, refill, 0)
        for store, cot, start, wide in kinds:
            base = spare if start == 0 else second + spare
            if start > 0 and between is not None:
                finish(between)
            for c in range(0, width, 128):
                row_t[c : c + 128, :] = rows[base : base + rows_e, c : c + 128].T
            for c in range(0, wide, COLUMN_TILE):
                cols = pl.ds(c, COLUMN_TILE)
                cots = cot[j * rows_e : (j + 1) * rows_e, cols]
                for low in range(0, n_dp, n_dp // 4):
                    some = row_t[low * share : (low + n_dp // 4) * share, :]
                    part = jnp.dot(some, cots, preferred_element_type=f32).astype(bf)
                    for r in range(low, low + n_dp // 4):
                        block = part[(r - low) * share : (r - low + 1) * share]
                        store[j, (r % 2) * half + r // 2, :, cols] = block
        for copy in to_sibling(j):
            copy.start()

    def one_pair(p, carry):
        arrive(2 * p + 1, token_rows)

        @pl.when(2 * p + 2 < n)
        def _():
            arrive(2 * p + 2, cotangents)

        sources = [source_of(2 * p), source_of(2 * p + 1)]
        for j in range(exp_dev):
            if j == exp_dev - 3:

                @pl.when(2 * p + 2 < n)
                def _():
                    arrive(2 * p + 2, token_rows)
                    arrive(2 * p + 3, cotangents)

            @pl.when(p == 0)
            def _():
                load_gu(j).wait()
                load_d(j).wait()

            gate_cols = []
            pair_a = pl.ds(j * pair, pair)
            pair_b = pl.ds(second + j * pair, pair)
            for s, src in enumerate(sources):
                here_a = pl.ds(j * pair + s * cap_p, cap_p)
                here_b = pl.ds(second + j * pair + s * cap_p, cap_p)
                hot, gate_col = scatter_slots(table_of(src), j, cap_p)
                gate_cols.append(gate_col)
                rows[here_a, :] = jnp.dot(hot, xg[src], preferred_element_type=f32).astype(bf)
                rows_dy = jnp.dot(hot, dyg[src], preferred_element_type=f32) * gate_col
                rows[here_b, :] = rows_dy.astype(bf)
            gate_col = jnp.concatenate(gate_cols, axis=0)
            w_in = wgu[j].reshape(width, 2 * hidden)
            w_out = wd[j].reshape(width, hidden)
            gate_up = jnp.dot(rows[pair_a, :], w_in, preferred_element_type=f32)
            inner_grad = jnp.dot(rows[pair_b, :], w_out, preferred_element_type=f32)
            gate_part = gate_up[:, :hidden]
            up_part = gate_up[:, hidden:]
            sig = jax.nn.sigmoid(gate_part)
            activated = gate_part * sig
            inner_act = (activated * up_part).astype(bf)
            grad_gate = inner_grad * up_part * sig * (1.0 + gate_part * (1.0 - sig))
            grad_up = inner_grad * activated
            grad_gu = jnp.concatenate([grad_gate, grad_up], axis=1).astype(bf)
            for s, src in enumerate(sources):
                place = pl.ds(pl.multiple_of(j * rows_e + src * cap_p, 16), cap_p)
                inner[place, :] = inner_act[s * cap_p : (s + 1) * cap_p]
                dgu[place, :] = grad_gu[s * cap_p : (s + 1) * cap_p]
            for c in range(0, width, BACK_TILE):
                rows_y = lax.dot_general(
                    inner_act,
                    w_out[c : c + BACK_TILE],
                    (((1,), (1,)), ((), ())),
                    preferred_element_type=f32,
                )
                rows[pair_a, pl.ds(c, BACK_TILE)] = (rows_y * gate_col).astype(bf)
            for c in range(0, width, BACK_TILE):
                rows_dx = lax.dot_general(
                    grad_gu,
                    w_in[c : c + BACK_TILE],
                    (((1,), (1,)), ((), ())),
                    preferred_element_type=f32,
                )
                rows[pair_b, pl.ds(c, BACK_TILE)] = rows_dx.astype(bf)
            if j <= early:

                @pl.when(p == n // 2 - 1)
                def _():
                    if j > 0:
                        finish(j - 1)
                    if j < early:
                        form(j)

        def hots_of(src):
            hots = [scatter_slots(table_of(src), j, cap_p)[0] for j in range(exp_dev)]
            return jnp.concatenate(hots, axis=0).T

        def slots_of(base, s, cols):
            parts = [rows[pl.ds(base + j * pair + s * cap_p, cap_p), cols] for j in range(exp_dev)]
            return jnp.concatenate(parts, axis=0)

        def outputs(s, hot_all):
            @pl.when(2 * p + s > 0)
            def _():
                mix_copy(2 * p + s - 1).wait()

            for c in range(0, width, COLUMN_TILE):
                cols = pl.ds(c, COLUMN_TILE)
                part = jnp.dot(hot_all, slots_of(0, s, cols), preferred_element_type=f32)
                mixs[:, cols] = part.astype(bf)
            mix_copy(2 * p + s).start()

        for s in (1, 0):
            src = sources[s]
            hot_all = hots_of(src)
            for c in range(0, width, COLUMN_TILE):
                cols = pl.ds(c, COLUMN_TILE)
                part = jnp.dot(hot_all, slots_of(second, s, cols), preferred_element_type=f32)
                dxs[src, :, cols] = part.astype(bf)
            if s == 0:

                @pl.when(p == 0)
                def _():
                    own_dx.start()

                @pl.when(p > 0)
                def _():
                    back(src).start()

                outputs(0, hot_all)
            else:
                back(src).start()
        outputs(1, hots_of(sources[1]))
        return carry

    lax.fori_loop(0, n // 2, one_pair, 0)

    for j in range(early, exp_dev):
        form(j, j - 1 if j > early else None)
    finish(exp_dev - 1)

    for k in range(1, n):
        peer = lax.rem(me + k, n)
        pltpu.make_async_remote_copy(
            src_ref=dxs.at[peer],
            dst_ref=dx_ref.at[peer],
            send_sem=back_send.at[peer],
            recv_sem=back_recv.at[peer],
            device_id={"expert": peer},
            device_id_type=MESH,
        ).wait_recv()
    for k in range(1, n):
        back(lax.rem(me + k, n)).wait_send()
    own_dx.wait()
    mix_copy(n - 1).wait()

    def settle(src, carry):
        for side in range(2):

            @pl.when(((src <= me) & (me < n - 1)) if side else ((src >= me) & (me > 0)))
            def _():
                for copy in hops(src, side, (0, 1, 2)):
                    copy.wait_send()

        return carry

    lax.fori_loop(0, n, settle, 0)
    for j in range(exp_dev):
        for copy in to_sibling(j) + to_plane(j):
            copy.wait_send()
        for copy in term_copies(j):
            copy.wait()
        for copy in to_plane(j):
            copy.wait_recv()


def run_layer(
    x, cot, w_qkv, w_out, w_gate_up, w_down, gain1, gain2, freq, doc_row, routes, gates, n, n_dp, capacity
):
    tok, width = x.shape
    exp_dev = w_gate_up.shape[0]
    hidden = w_down.shape[2]
    cap_p = -(-capacity // 16) * 16
    share = width // n_dp
    bf = jnp.bfloat16
    f32 = jnp.float32
    rows_e = n * cap_p
    spec = pl.BlockSpec(memory_space=pltpu.VMEM)
    any_spec = pl.BlockSpec(memory_space=pl.ANY)
    dma = pltpu.SemaphoreType.DMA
    macs = rows_e * exp_dev * width * hidden * 9 + tok * width * (w_qkv.shape[1] + width)
    shapes = (
        (tok, HEADS * HD),
        (tok, KV * HD),
        (tok, KV * HD),
        (tok, HEADS * HD),
        (n, tok, width),
        (n, tok, width),
        (n_dp // 2, exp_dev, share, 3 * hidden),
        (2, n_dp // 4, exp_dev, share // 2, 3 * hidden),
        (exp_dev, n_dp // 2, share, 2 * hidden),
        (exp_dev, n_dp // 2, share, hidden),
    )
    return pl.pallas_call(
        functools.partial(layer_kernel, n, exp_dev, cap_p),
        out_shape=tuple(jax.ShapeDtypeStruct(shape, bf) for shape in shapes),
        in_specs=[any_spec] * 6 + [spec] * 6,
        out_specs=(any_spec,) * len(shapes),
        scratch_shapes=[
            pltpu.VMEM((exp_dev, n_dp, share, 2 * hidden), bf),
            pltpu.VMEM((exp_dev, n_dp, share, hidden), bf),
            pltpu.VMEM((n, tok, width), bf),
            pltpu.VMEM((n, n * TABLE_ROWS, tok), f32),
            pltpu.VMEM((n, tok, width), bf),
            pltpu.VMEM((exp_dev * rows_e, 2 * hidden), bf),
            pltpu.VMEM((exp_dev * rows_e, hidden), bf),
            pltpu.VMEM((max(4 * exp_dev * cap_p, width), width), bf),
            pltpu.VMEM((width, rows_e), bf),
            pltpu.VMEM((n, tok, width), bf),
            pltpu.VMEM((tok, width), bf),
            dma((3,)),
            dma((8,)),
            dma((2, exp_dev)),
            dma((3, 2, n)),
            dma((3, n)),
            dma((n,)),
            dma((n,)),
            dma((2, exp_dev)),
            dma((1,)),
            dma((2, exp_dev)),
            dma((2, exp_dev)),
            dma((2, 2, n_dp // 4, exp_dev)),
            dma((2, 2, n_dp // 4, exp_dev)),
            dma((n_dp,)),
        ],
        compiler_params=pltpu.CompilerParams(
            collective_id=0, has_side_effects=True, vmem_limit_bytes=127 * 512 * 1024
        ),
        cost_estimate=pl.CostEstimate(
            flops=2 * macs,
            bytes_accessed=64 * 1024 * 1024,
            transcendentals=rows_e * exp_dev * hidden + HEADS * tok * tok,
        ),
    )(
        x,
        cot,
        w_qkv,
        w_out,
        w_gate_up.reshape(exp_dev, n_dp, share, 2 * hidden),
        w_down.reshape(exp_dev, n_dp, share, hidden),
        gain1,
        gain2,
        freq,
        doc_row,
        routes,
        gates,
    )


def tail_kernel(n, n_dp, exp_dev, *refs):
    dx_ref, mix_ref, term_ref, land_ref, wq_ref, wo_ref = refs[:6]
    dy_ref, x_ref, q_ref, k_ref, v_ref, o_ref = refs[6:12]
    freq_ref, row_ref, gain1_ref, gain2_ref = refs[12:16]
    gx_ref, h2_keep, r3, u3, y_land, own_last, got_last = refs[16:23]
    weight, parts, do, dqk, dh2_ref, gains, acc, got = refs[23:31]
    lhs, rhs, s1, r1, r2, s2, t1, u1, u2, t2 = refs[31:41]
    load_sem, piece_sem, y_send, y_recv, step_send, step_recv, out_sem, own_sem = refs[41:49]
    pair_send, pair_recv, dp_send, dp_recv, ex_send, ex_recv = refs[49:]
    dp = lax.axis_index("dp")
    me = lax.axis_index("expert")
    core = lax.rem(dp, 2)
    q = lax.div(dp, 2)
    half = n_dp // 2
    steps = half.bit_length() - 1
    f32 = jnp.float32
    bf = jnp.bfloat16
    tok, width = x_ref.shape
    rows = width // (n * n_dp)
    q_cols = HEADS * HD
    k_cols = KV * HD
    qkv = q_cols + 2 * k_cols
    out_chunks = width // CHUNK
    chunks = out_chunks + qkv // CHUNK
    ring = s1.shape[0]
    group = HEADS // KV
    scale = 1.0 / math.sqrt(HD)
    wide = (((1,), (1,)), ((), ()))
    tall = (((0,), (0,)), ((), ()))
    sibling = {"dp": dp + 1 - 2 * core}
    cut, span = acc.shape[3:]

    def value(bit):
        return lax.rem(lax.div(q, 1 << bit), 2)

    def across(bit):
        return {"dp": 2 * (q + (1 - 2 * value(bit)) * (1 << bit)) + core}

    def ex_peer(k):
        return lax.rem(me + k, n)

    batch = parts.shape[0] // tok
    h2_ref = dqk.at[:, pl.ds(0, width)]
    h2_out = pltpu.make_async_copy(h2_ref, h2_keep, load_sem.at[n + 2])

    def part_load(src, k):
        return pltpu.make_async_copy(src, parts.at[pl.ds(k % batch * tok, tok)], load_sem.at[k])

    def part(k):
        return parts[k % batch * tok : (k % batch + 1) * tok, :].astype(f32)

    dx_loads = [part_load(dx_ref.at[k], k) for k in range(n)]
    load_o = pltpu.make_async_copy(wo_ref, weight.at[:, pl.ds(0, width)], load_sem.at[n])
    load_q = pltpu.make_async_copy(wq_ref, weight, load_sem.at[n + 1])
    load_o.start()

    def kept_load(side, t):
        low = t % (1 << side)
        block = (t - low) * 2 + value(side) * (1 << side) + low
        return pltpu.make_async_copy(
            term_ref.at[block, :, pl.ds(side * cut, cut), :],
            acc.at[side, t],
            piece_sem.at[side, t, exp_dev],
        )

    def land_load(side, t, e):
        return pltpu.make_async_copy(
            land_ref.at[side, t, e],
            parts.at[pl.ds((t * exp_dev + e) * cut, cut)],
            piece_sem.at[side, t, e],
        )

    for side in range(2):
        for t in range(half // 2):
            kept_load(side, t).start()
    for t in range(half // 2):
        for e in range(exp_dev):
            land_load(0, t, e).start()

    barrier = pltpu.get_barrier_semaphore()
    pl.semaphore_signal(barrier, inc=1, device_id=sibling, device_id_type=MESH)
    for bit in range(steps):
        pl.semaphore_signal(barrier, inc=1, device_id=across(bit), device_id_type=MESH)
    for k in range(1, n):
        pl.semaphore_signal(
            barrier, inc=1, device_id={"expert": ex_peer(k)}, device_id_type=MESH
        )
    pl.semaphore_wait(barrier, 1 + steps + (n - 1))

    def y_copy(peer, slot):
        return pltpu.make_async_remote_copy(
            src_ref=mix_ref.at[peer],
            dst_ref=y_land.at[slot],
            send_sem=y_send.at[peer],
            recv_sem=y_recv.at[slot],
            device_id={"expert": peer},
            device_id_type=MESH,
        )

    for k in range(1, n):
        y_copy(ex_peer(k), me).start()

    def lands(side):
        return [land_load(side, t, e) for t in range(half // 2) for e in range(exp_dev)]

    def step_order(side):
        return [bit for bit in reversed(range(steps)) if bit != side]

    def step_start(side, s):
        order = step_order(side)[:s]
        return sum(value(bit) * (half >> (t + 2)) for t, bit in enumerate(order))

    def step_copy(side, s):
        bit = step_order(side)[s]
        size = half >> (s + 2)
        start = step_start(side, s) + (1 - value(bit)) * size
        return pltpu.make_async_remote_copy(
            src_ref=acc.at[side, pl.ds(start, size)],
            dst_ref=got.at[side, pl.ds(half // 2 - 2 * size, size)],
            send_sem=step_send.at[side, s],
            recv_sem=step_recv.at[side, s],
            device_id=across(bit),
            device_id_type=MESH,
        )

    def last_copy(side, part):
        bit = step_order(side)[steps - 2]
        start = step_start(side, steps - 2) + 1 - value(bit)
        experts = pl.ds(2, exp_dev - 2) if part else pl.ds(0, 2)
        return pltpu.make_async_remote_copy(
            src_ref=acc.at[side, start, experts],
            dst_ref=got_last.at[experts, side],
            send_sem=step_send.at[side, steps - 2 + part],
            recv_sem=step_recv.at[side, steps - 2 + part],
            device_id=across(bit),
            device_id_type=MESH,
        )

    def start_step(side, s):
        if s < steps - 2:
            step_copy(side, s).start()
        else:
            last_copy(side, 0).start()
            last_copy(side, 1).start()

    def first_step(side):
        for t in range(half // 2):
            kept_load(side, t).wait()
        for copy in lands(side):
            copy.wait()
        for t in range(half // 2):
            for e in range(exp_dev):
                piece = parts[(t * exp_dev + e) * cut : (t * exp_dev + e + 1) * cut, :]
                acc[side, t, e] += piece
        start_step(side, 0)

    def next_steps(side):
        for s in range(steps - 2):
            step_copy(side, s).wait_recv()
            size = half >> (s + 2)
            start = step_start(side, s + 1)
            for b in range(size):
                acc[side, start + b] += got[side, half // 2 - 2 * size + b]
            start_step(side, s + 1)

    def own_share(side):
        start = step_start(side, steps - 1)
        return pltpu.make_async_copy(acc.at[side, start], own_last.at[:, side], out_sem.at[side])

    def bufs(c):
        if c is None:
            return t1, u1, u2, t2, u3, chunks
        return s1.at[c % ring], r1.at[c], r2.at[c], s2.at[c], r3.at[:, :, pl.ds(c * CHUNK, CHUNK)], c

    def to_sibling(c):
        mine, landed, _, _, _, i = bufs(c)
        return pltpu.make_async_remote_copy(
            src_ref=mine.at[1 - core],
            dst_ref=landed,
            send_sem=pair_send.at[i],
            recv_sem=pair_recv.at[i],
            device_id=sibling,
            device_id_type=MESH,
        )

    def order_of(c):
        bits = list(range(steps))
        return bits[::-1] if c is not None and c % 2 else bits

    def position(place, c):
        order = order_of(c)
        return sum(((place >> bit) & 1) << (len(order) - 1 - s) for s, bit in enumerate(order))

    def start_of(c, s):
        order = order_of(c)
        return sum(value(bit) * (half >> (t + 1)) for t, bit in enumerate(order[:s]))

    def to_plane(c, s):
        mine, _, landed, _, _, i = bufs(c)
        bit = order_of(c)[s]
        size = half >> (s + 1)
        start = start_of(c, s) + (1 - value(bit)) * size
        return pltpu.make_async_remote_copy(
            src_ref=mine.at[core, pl.ds(start, size)],
            dst_ref=landed.at[pl.ds(half - 2 * size, size)],
            send_sem=dp_send.at[i, s],
            recv_sem=dp_recv.at[i, s],
            device_id=across(bit),
            device_id_type=MESH,
        )

    def to_expert(c, peer, slot):
        _, _, _, mine, landed, i = bufs(c)
        return pltpu.make_async_remote_copy(
            src_ref=mine.at[peer],
            dst_ref=landed.at[slot],
            send_sem=ex_send.at[i, peer],
            recv_sem=ex_recv.at[i, slot],
            device_id={"expert": peer},
            device_id_type=MESH,
        )

    def sent(c):
        to_sibling(c).wait_send()
        for s in range(steps):
            to_plane(c, s).wait_send()

    def place(c):
        if c is None:
            padding = jnp.zeros((GAIN_ROWS - gains.shape[0], width), f32)
            term = jnp.concatenate([gains[...], padding], axis=0).T
        else:
            if c >= ring:
                sent(c - ring)
            side = 0 if c < out_chunks else 1
            term = jnp.dot(lhs[side], rhs[c], preferred_element_type=f32)
        mine = bufs(c)[0]
        for b in range(n_dp * n):
            d, e = divmod(b, n)
            block = term[b * rows : (b + 1) * rows].astype(mine.dtype)
            mine[d % 2, position(d // 2, c), e, 0:rows, :] = block
        to_sibling(c).start()

    def pair_up(c):
        to_sibling(c).wait_recv()
        mine, landed = bufs(c)[:2]
        for b in range(half):
            mine[core, b] += landed[b]
        to_plane(c, 0).start()

    def halve(c, s):
        to_plane(c, s).wait_recv()
        mine, _, landed, summed = bufs(c)[:4]
        size = half >> (s + 1)
        start = start_of(c, s + 1)
        for b in range(size):
            both = mine[core, start + b] + landed[half - 2 * size + b]
            if s + 1 < steps:
                mine[core, start + b] = both
            else:
                summed[...] = both
        if s + 1 < steps:
            to_plane(c, s + 1).start()
        else:
            own_sum(c).start()
            for k in range(1, n):
                to_expert(c, ex_peer(k), me).start()

    def own_sum(c):
        summed, landed, i = bufs(c)[3:]
        return pltpu.make_async_copy(summed.at[me], landed.at[me], own_sem.at[i])

    def last(c):
        for k in range(1, n):
            to_expert(c, ex_peer(k), ex_peer(k)).wait_recv()

    first_step(0)
    for copy in lands(1):
        copy.start()
    gains[...] = jnp.zeros_like(gains)
    load_o.wait()
    for c in range(0, width, CHUNK):
        cols = slice(c, c + CHUNK)
        a = jnp.dot(o_ref[...], weight[:, cols], preferred_element_type=f32)
        h2_ref[:, cols] = x_ref[:, cols].astype(f32) + a
    h2_out.start()
    first_step(1)
    for copy in dx_loads[:batch]:
        copy.start()
    lhs[0] = o_ref[...].T
    for first in range(0, n, batch):
        for copy in dx_loads[first : first + batch]:
            if first > 0:
                copy.start()
        for copy in dx_loads[first : first + batch]:
            copy.wait()
        total = part(first)
        for k in range(first + 1, min(first + batch, n)):
            total = total + part(k)
        dh2_ref[...] = total if first == 0 else dh2_ref[...] + total
    h2 = h2_ref[...]
    dxn2 = dh2_ref[...]
    r2_col = inverse_rms(h2)
    gains[1:2, :] = jnp.sum(dxn2 * h2 * r2_col, axis=0, keepdims=True)
    w2 = dxn2 * gain2_ref[...]
    cubed = r2_col**3 * jnp.mean(w2 * h2, axis=1, keepdims=True)
    dh2_ref[...] = dy_ref[...].astype(f32) + r2_col * w2 - h2 * cubed
    for c in range(out_chunks):
        rhs[c] = dh2_ref[:, c * CHUNK : (c + 1) * CHUNK].astype(bf)
    for c in range(out_chunks):
        place(c)
    for c in range(0, q_cols, CHUNK):
        total = jnp.zeros((tok, CHUNK), f32)
        for d in range(out_chunks):
            total = total + lax.dot_general(
                rhs[d],
                weight[c : c + CHUNK, d * CHUNK : (d + 1) * CHUNK],
                wide,
                preferred_element_type=f32,
            )
        do[:, c : c + CHUNK] = total.astype(bf)
    load_q.start()
    for c in range(out_chunks):
        pair_up(c)

    h2_out.wait()
    cos_t, sin_t, mask = rotary(row_ref[...], freq_ref[...])
    mask3 = jnp.concatenate([mask] * group, axis=0)

    def put_proj(first, block):
        c, rest = divmod(first, CHUNK)
        rhs[out_chunks + c, :, rest : rest + block.shape[1]] = block

    for g in range(KV):
        q3 = heads_of(q_ref, g * group, group)
        k1 = heads_of(k_ref, g, 1)
        v1 = heads_of(v_ref, g, 1)
        do3 = heads_of(do, g * group, group)
        weights = softmax_parts(masked_scores(q3, k1, mask3))
        dpr = lax.dot_general(do3, v1, wide, preferred_element_type=f32)
        delta = jnp.sum(dpr * weights, axis=1, keepdims=True)
        ds = (weights * (dpr - delta)).astype(bf)
        dq = jnp.dot(ds, k1, preferred_element_type=f32) * scale
        for s in range(group):
            first = (g * group + s) * HD
            dqk[:, first : first + HD] = dq[s * tok : (s + 1) * tok]
        first = q_cols + g * HD
        dqk[:, first : first + HD] = (
            lax.dot_general(ds, q3, tall, preferred_element_type=f32) * scale
        )
        dv = lax.dot_general(weights.astype(bf), do3, tall, preferred_element_type=f32)
        put_proj(q_cols + k_cols + g * HD, dv.astype(bf))
    for c in range(0, q_cols + k_cols, 128):
        tile = dqk[:, c : c + 128]
        turned = halves(tile * sin_t, -1.0)
        put_proj(c, (tile * cos_t + turned).astype(bf))
    h = x_ref[...].astype(f32)
    r1_col = inverse_rms(h)
    lhs[1] = (h * r1_col * gain1_ref[...]).astype(bf).T

    def first_norm():
        load_q.wait()
        dxn1 = jnp.zeros((tok, width), f32)
        for c in range(out_chunks, chunks):
            first = (c - out_chunks) * CHUNK
            dxn1 = dxn1 + lax.dot_general(
                rhs[c], weight[:, first : first + CHUNK], wide, preferred_element_type=f32
            )
        x = x_ref[...].astype(f32)
        gains[0:1, :] = jnp.sum(dxn1 * x * r1_col, axis=0, keepdims=True)
        w1 = dxn1 * gain1_ref[...]
        cubed = r1_col**3 * jnp.mean(w1 * x, axis=1, keepdims=True)
        gx_ref[...] = (dh2_ref[...] + r1_col * w1 - x * cubed).astype(bf)

    line = list(range(chunks)) + [None]
    late = line[out_chunks:]
    for tick in range(len(line) + steps):
        for s in reversed(range(steps)):
            if 0 <= tick - s < len(line):
                halve(line[tick - s], s)
        if tick < len(late):
            place(late[tick])
        if 1 <= tick <= len(late):
            pair_up(late[tick - 1])
        if 0 <= tick - steps < len(line):
            last(line[tick - steps])
        if tick == 1:
            first_norm()
        if tick == 3:
            for side in range(2):
                next_steps(side)
                own_share(side).start()

    for c in line:
        if c is None or c >= chunks - ring:
            sent(c)
        for k in range(1, n):
            to_expert(c, ex_peer(k), me).wait_send()
    for c in line:
        own_sum(c).wait()
    for side in range(2):
        for s in range(steps - 2):
            step_copy(side, s).wait_send()
        for half_of in range(2):
            last_copy(side, half_of).wait()
        own_share(side).wait()
    for k in range(1, n):
        y_copy(ex_peer(k), ex_peer(k)).wait_recv()
        y_copy(ex_peer(k), me).wait_send()


def run_tail(
    dx_parts, mix_parts, term, landed, w_qkv, w_out, dy, x, q, k, v, o, freq, doc_row, gain1, gain2, n, n_dp
):
    tok, width = x.shape
    exp_dev = term.shape[1]
    cut, span = landed.shape[3:]
    qkv = w_qkv.shape[1]
    rows = width // (n * n_dp)
    rows_p = -(-rows // 16) * 16
    half = n_dp // 2
    steps = half.bit_length() - 1
    chunks = (width + qkv) // CHUNK
    ring = steps + 2
    lanes = GAIN_ROWS
    bf = jnp.bfloat16
    f32 = jnp.float32
    dma = pltpu.SemaphoreType.DMA
    spec = pl.BlockSpec(memory_space=pltpu.VMEM)
    any_spec = pl.BlockSpec(memory_space=pl.ANY)
    return pl.pallas_call(
        functools.partial(tail_kernel, n, n_dp, exp_dev),
        out_shape=(
            jax.ShapeDtypeStruct((tok, width), bf),
            jax.ShapeDtypeStruct((tok, width), f32),
            jax.ShapeDtypeStruct((n, rows_p, chunks * CHUNK), bf),
            jax.ShapeDtypeStruct((n, rows_p, lanes), f32),
            jax.ShapeDtypeStruct((n, tok, width), bf),
            jax.ShapeDtypeStruct((exp_dev, 2, cut, span), bf),
            jax.ShapeDtypeStruct((exp_dev, 2, cut, span), bf),
        ),
        in_specs=[any_spec] * 6 + [spec] * 10,
        out_specs=(spec,) + (any_spec,) * 6,
        scratch_shapes=[
            pltpu.VMEM((width, qkv), bf),
            pltpu.VMEM((min(n, 4) * tok, width), bf),
            pltpu.VMEM((tok, HEADS * HD), bf),
            pltpu.VMEM((tok, (HEADS + KV) * HD), f32),
            pltpu.VMEM((tok, width), f32),
            pltpu.VMEM((8, width), f32),
            pltpu.VMEM((2, half // 2, exp_dev, cut, span), bf),
            pltpu.VMEM((2, max(half // 2 - 2, 1), exp_dev, cut, span), bf),
            pltpu.VMEM((2, width, tok), bf),
            pltpu.VMEM((chunks, tok, CHUNK), bf),
            pltpu.VMEM((ring, 2, half, n, rows_p, CHUNK), bf),
            pltpu.VMEM((chunks, half, n, rows_p, CHUNK), bf),
            pltpu.VMEM((chunks, half - 1, n, rows_p, CHUNK), bf),
            pltpu.VMEM((chunks, n, rows_p, CHUNK), bf),
            pltpu.VMEM((2, half, n, rows_p, lanes), f32),
            pltpu.VMEM((half, n, rows_p, lanes), f32),
            pltpu.VMEM((half - 1, n, rows_p, lanes), f32),
            pltpu.VMEM((n, rows_p, lanes), f32),
            dma((n + 3,)),
            dma((2, half // 2, exp_dev + 1)),
            dma((n,)),
            dma((n,)),
            dma((2, steps)),
            dma((2, steps)),
            dma((2,)),
            dma((chunks + 1,)),
            dma((chunks + 1,)),
            dma((chunks + 1,)),
            dma((chunks + 1, steps)),
            dma((chunks + 1, steps)),
            dma((chunks + 1, n)),
            dma((chunks + 1, n)),
        ],
        compiler_params=pltpu.CompilerParams(
            collective_id=1, has_side_effects=True, vmem_limit_bytes=127 * 512 * 1024
        ),
        cost_estimate=pl.CostEstimate(
            flops=2 * tok * width * (3 * qkv + 3 * width),
            bytes_accessed=64 * 1024 * 1024,
            transcendentals=HEADS * tok * tok,
        ),
    )(dx_parts, mix_parts, term, landed, w_qkv, w_out, dy, x, q, k, v, o, freq, doc_row, gain1, gain2)


def shards(
    layer_input,
    gain_attn,
    w_qkv,
    w_out,
    gain_moe,
    w_gate_up,
    w_down,
    doc_ids,
    routes,
    gates,
    cotangent,
):
    tok_rows, model_width = layer_input.shape
    exp_dev = w_gate_up.shape[0]
    top_count = routes.shape[1]
    owners = lax.axis_size("expert")
    n_dp = lax.axis_size("dp")
    n_experts = exp_dev * owners
    capacity = 8 * (3 * tok_rows * top_count // (16 * n_experts))
    lane = np.arange(128) % (HD // 2)
    freq = jnp.asarray((ROPE_BASE ** (-(lane * 2.0 / HD)))[None].astype(np.float32))
    gain1 = gain_attn.reshape(1, model_width)
    gain2 = gain_moe.reshape(1, model_width)
    q, k, v, attended, grad_partial, mix_partial, term, landed, *_ = run_layer(
        layer_input,
        cotangent,
        w_qkv,
        w_out,
        w_gate_up,
        w_down,
        gain1,
        gain2,
        freq,
        doc_ids,
        routes.T,
        gates.T,
        owners,
        n_dp,
        capacity,
    )
    grad_x, middle, dense, gain_parts, mix_landed, own_share, got_share = run_tail(
        grad_partial,
        mix_partial,
        term,
        landed,
        w_qkv,
        w_out,
        cotangent,
        layer_input,
        q,
        k,
        v,
        attended,
        freq,
        doc_ids,
        gain1,
        gain2,
        owners,
        n_dp,
    )
    f32 = jnp.float32
    me = lax.axis_index("expert")
    hidden = w_down.shape[2]
    share_rows = model_width // (owners * n_dp)
    mixture = lax.dynamic_index_in_dim(mix_partial, me, 0, keepdims=False).astype(f32)
    for k in range(1, owners):
        peer = (me + k) % owners
        mixture = mixture + lax.dynamic_index_in_dim(mix_landed, peer, 0, keepdims=False).astype(f32)
    layer_output = (middle + mixture).astype(jnp.bfloat16)
    gain_share = jnp.sum(gain_parts[:, :share_rows], axis=0)

    def dense_sum(first, last):
        return jnp.sum(dense[:, :share_rows, first:last].astype(f32), axis=0)

    def expert_sum(first, last):
        total = own_share[..., first:last].astype(f32) + got_share[..., first:last].astype(f32)
        return total.reshape(w_down.shape[0], model_width // n_dp, last - first)

    return (
        layer_output,
        grad_x,
        gain_share[:, 0],
        dense_sum(model_width, dense.shape[2]),
        dense_sum(0, model_width),
        gain_share[:, 1],
        expert_sum(0, 2 * hidden),
        expert_sum(2 * hidden, 3 * hidden),
    )


def solution(mesh):
    in_specs = (
        P(("dp", "expert"), None),
        P(),
        P(),
        P(),
        P(),
        P("expert", None, None),
        P("expert", None, None),
        P(("dp", "expert"), None),
        P(("dp", "expert"), None),
        P(("dp", "expert"), None),
        P(("dp", "expert"), None),
    )
    out_specs = (
        P(("dp", "expert"), None),
        P(("dp", "expert"), None),
        P(("dp", "expert")),
        P(("dp", "expert"), None),
        P(("dp", "expert"), None),
        P(("dp", "expert")),
        P("expert", "dp", None),
        P("expert", "dp", None),
    )
    return jax.shard_map(shards, mesh=mesh, in_specs=in_specs, out_specs=out_specs, check_vma=False)
```
